32 devices in a mesh: gx: 2 (over y), gy: 16 (over z, x, core).
Axes of the slice: x: 2, y: 2, z: 4, core: 2. Of those that a mesh axis runs over, the one named last changes fastest.
Arguments:
- disp: bfloat16 [10, 160, 26, 3], P('gx', 'gy'), may hold values from -6 to 6
- disp_prev: bfloat16 [10, 160, 26, 3], P('gx', 'gy'), may hold values from -6 to 6
- tangent: bfloat16 [10, 160, 4992], P('gx', 'gy'), may hold values from -6 to 6
- tangent_prev: bfloat16 [10, 160, 4992], P('gx', 'gy'), may hold values from -6 to 6
- lame_lambda: bfloat16 [2, 32, 5], P('gx', 'gy'), may hold values from 0.29882812 to 3
- lame_mu: bfloat16 [2, 32, 5], P('gx', 'gy'), may hold values from 0.29882812 to 3
- node_mass: float32 [10, 160, 26], P('gx', 'gy'), may hold values from 0.5 to 2
- force: bfloat16 [10, 160, 26, 3], P('gx', 'gy'), may hold values from -48 to 48
- cell_block: int32 [2, 32, 5], P('gx', 'gy'), may hold values from 0 to 63
- direction_block: int32 [64], replicated, may hold values from 0 to 63
- port_id: int32 [10, 160, 26], P('gx', 'gy'), may hold values from 0 to 64, as said below
- port_mode: bfloat16 [10, 160, 26, 3], P('gx', 'gy'), may hold values from -0.059814453 to 0.059814453
Outputs:
- disp_next: bfloat16 [10, 160, 26, 3], P('gx', 'gy')
- tangent_next: bfloat16 [10, 160, 4992], P('gx', 'gy')
- port_amp: float32 [64, 64], P('gy', 'gx')
The draws below stay inside these ranges and needn't reach their ends.
Inputs may be any that keep to these rules, and one draw needn't show every extreme that they name: `port_id`: 64 marks a node outside every output section; the output sections are the last 40 node layers along the second dimension, where every node belongs to some port; within each node line along the first dimension the port numbers never fall.
All inputs are finite; a program needn't handle non-finite values.
Results may differ from the reference program's by a relative error of at most 0.0016.
Values may be sent and summed in bfloat16 or wider, within the bound.
A program may use at most 192 MiB of HBM per device.

```python
import math
import jax
import jax.numpy as jnp
import numpy as np
from jax import lax

EZ = 5
NT = 64
PORTS = 64
BLOCKS = 64
PORT_DEPTH = 40
EXG = 2
EYG = 32
NXN = 10
NYN = 160
NZN = 26


def draw_port_id(key, part):
    key = jax.random.fold_in(key, 11)
    shift_key = jax.random.fold_in(key, 1)
    phase_key = jax.random.fold_in(key, 2)
    reach = max(1, NXN // 4)
    edge_shift = jax.random.randint(shift_key, (1, NYN, NZN), -reach, reach + 1, dtype=jnp.int32)
    phase = jax.random.randint(phase_key, (1, NYN, NZN), 0, NXN, dtype=jnp.int32)
    layer_index = jnp.arange(NXN, dtype=jnp.int32)[:, None, None]
    banded = jnp.clip(((layer_index + edge_shift) * PORTS + phase) // NXN, 0, PORTS - 1)
    row_index = jnp.arange(NYN, dtype=jnp.int32)[None, :, None]
    return jnp.where(row_index >= NYN - PORT_DEPTH, banded, PORTS).astype(jnp.int32)


def touch_ends(entries, stream_key, smallest, largest):
    dims = entries.shape
    spot = [jax.random.randint(jax.random.fold_in(stream_key, axis), (), 0, dims[axis]) for axis in range(len(dims))]
    entries = entries.at[tuple(spot)].set(smallest)
    longest = dims.index(max(dims))
    spot[longest] = (spot[longest] + 1) % dims[longest]
    return entries.at[tuple(spot)].set(largest)


def block_levels(stream_key, dims, cuts, smallest, high):
    loudness, own = 1.0, jax.random.fold_in(stream_key, 6)
    for position, parts in cuts:
        steps = jnp.exp(jax.random.uniform(jax.random.fold_in(own, position), (parts,), jnp.float32, smallest / len(cuts), high / len(cuts)))
        loudness = loudness * jnp.repeat(steps, dims[position] // parts).reshape([-1 if axis == position else 1 for axis in range(len(dims))])
    return loudness


def gaussian(stream_key, shape, width, limit, split=(), kind=jnp.bfloat16):
    values = width * jax.random.normal(stream_key, shape, jnp.float32)
    if split:
        values = values * block_levels(stream_key, shape, split, -0.22, 0.18)
    return jnp.clip(values, -limit, limit).astype(kind)


def setup_inputs(seed: int = 0) -> dict:
    seeds = jax.random.split(jax.random.key(seed), 13)
    disp = gaussian(seeds[0], (NXN, NYN, NZN, 3), 1.0, 6.0, ((0, 2), (1, 16)))
    disp_prev = gaussian(seeds[1], (NXN, NYN, NZN, 3), 1.0, 6.0, ((0, 2), (1, 16)))
    tangent = gaussian(seeds[2], (NXN, NYN, NZN * 3 * NT), 1.0, 6.0, ((0, 2), (1, 16)))
    tangent_prev = gaussian(seeds[3], (NXN, NYN, NZN * 3 * NT), 1.0, 6.0, ((0, 2), (1, 16)))
    lame_lambda = jnp.clip(jnp.exp(math.log(3.0) - 2.306499 * jax.random.uniform(seeds[4], (EXG, EYG, EZ), jnp.float32) ** block_levels(seeds[4], (EXG, EYG, EZ), ((0, 2), (1, 16)), -0.2, 0.2)), 0.29882812, 3.0).astype(jnp.bfloat16)
    lame_mu = jnp.clip(jnp.exp(math.log(3.0) - 2.306499 * jax.random.uniform(seeds[5], (EXG, EYG, EZ), jnp.float32) ** block_levels(seeds[5], (EXG, EYG, EZ), ((0, 2), (1, 16)), -0.2, 0.2)), 0.29882812, 3.0).astype(jnp.bfloat16)
    node_mass = jnp.clip(jnp.exp(math.log(2.0) - 1.3862944 * jax.random.uniform(seeds[6], (NXN, NYN, NZN), jnp.float32) ** block_levels(seeds[6], (NXN, NYN, NZN), ((0, 2), (1, 16)), -0.2, 0.2)), 0.5, 2.0)
    force = gaussian(seeds[7], (NXN, NYN, NZN, 3), 8.0, 48.0, ((0, 2), (1, 16)))
    cell_block = touch_ends(jax.random.randint(seeds[8], (EXG, EYG, EZ), 0, BLOCKS), jax.random.fold_in(seeds[8], 1), 0, BLOCKS - 1).astype(jnp.int32)
    direction_block = touch_ends(jax.random.randint(seeds[9], (NT,), 0, BLOCKS), jax.random.fold_in(seeds[9], 1), 0, BLOCKS - 1).astype(jnp.int32)
    port_id = draw_port_id(jax.random.fold_in(seeds[12], 71), 0)
    port_mode = gaussian(seeds[11], (NXN, NYN, NZN, 3), 0.01, 0.059814453, ((0, 2), (1, 16)))
    return dict(disp=disp, disp_prev=disp_prev, tangent=tangent, tangent_prev=tangent_prev, lame_lambda=lame_lambda, lame_mu=lame_mu, node_mass=node_mass, force=force, cell_block=cell_block, direction_block=direction_block, port_id=port_id, port_mode=port_mode)


GLL_POINTS = np.array([-1.0, -0.765055323929465, -0.285231516480645, 0.285231516480645, 0.765055323929465, 1.0])
GLL_WEIGHTS = np.array([1.0 / 15.0, 0.378474956297847, 0.554858377035486, 0.554858377035486, 0.378474956297847, 1.0 / 15.0])
STEP_SQUARED = 0.03
HIGHEST = lax.Precision.HIGHEST
BACK_FORMS = ("pa,xpybzcn->xaybzcn", "pb,xaypzcn->xaybzcn", "pc,xaybzpn->xaybzcn")


def derivative_table():
    identity = np.eye(6)
    differences = GLL_POINTS[:, None] - GLL_POINTS[None, :] + identity
    barycentric = 1.0 / np.prod(differences, axis=1)
    matrix = (barycentric[None, :] / barycentric[:, None]) / differences
    matrix = matrix * (1.0 - identity)
    matrix = matrix - identity * matrix.sum(axis=1)[:, None]
    return matrix


def point_weights():
    cubed = GLL_WEIGHTS[:, None, None] * GLL_WEIGHTS[None, :, None] * GLL_WEIGHTS[None, None, :]
    return jnp.asarray(cubed.reshape(1, 6, 1, 6, 1, 6, 1), jnp.float32)


def split_axis(values, axis_at):
    values = jnp.moveaxis(values, axis_at, 0)
    elem_count = (values.shape[0] - 1) // 5
    main_part = values[:5 * elem_count].reshape((elem_count, 5) + values.shape[1:])
    tail_part = values[5::5][:, None]
    joined = jnp.concatenate([main_part, tail_part], axis=1)
    return jnp.moveaxis(joined, (0, 1), (axis_at, axis_at + 1))


def merge_axis(values, axis_at):
    values = jnp.moveaxis(values, (axis_at, axis_at + 1), (0, 1))
    elem_count = values.shape[0]
    rest_shape = values.shape[2:]
    main_part = values[:, :5].reshape((5 * elem_count,) + rest_shape)
    main_part = jnp.concatenate([main_part, jnp.zeros((1,) + rest_shape, values.dtype)], axis=0)
    tail_part = jnp.concatenate([values[:, 5:6], jnp.zeros((elem_count, 4) + rest_shape, values.dtype)], axis=1)
    tail_part = tail_part.reshape((5 * elem_count,) + rest_shape)
    tail_part = jnp.concatenate([jnp.zeros((5,) + rest_shape, values.dtype), tail_part], axis=0)[:5 * elem_count + 1]
    return jnp.moveaxis(main_part + tail_part, 0, axis_at)


def to_cells(values):
    return split_axis(split_axis(split_axis(values, 0), 2), 4)


def to_nodes(values):
    return merge_axis(merge_axis(merge_axis(values, 4), 2), 0)


def gradients(cells, deriv):
    return [
        jnp.einsum("pa,xaybzcn->xpybzcn", deriv, cells, precision=HIGHEST),
        jnp.einsum("pb,xaybzcn->xaypzcn", deriv, cells, precision=HIGHEST),
        jnp.einsum("pc,xaybzcn->xaybzpn", deriv, cells, precision=HIGHEST),
    ]


def internal_forces(gradient_list, lam_cells, mu_cells, deriv, weights, block_width):
    def column_block(values, component):
        return values[..., component * block_width:(component + 1) * block_width]

    dilation = column_block(gradient_list[0], 0) + column_block(gradient_list[1], 1) + column_block(gradient_list[2], 2)
    summed = None
    for direction in range(3):
        pieces = []
        for component in range(3):
            stress = mu_cells * (column_block(gradient_list[direction], component) + column_block(gradient_list[component], direction))
            if component == direction:
                stress = stress + lam_cells * dilation
            pieces.append(weights * stress)
        contribution = jnp.einsum(BACK_FORMS[direction], deriv, jnp.concatenate(pieces, axis=-1), precision=HIGHEST)
        summed = contribution if summed is None else summed + contribution
    return summed


def block_forces(primal_nodes, tangent_nodes, lam_cells, mu_cells, select):
    deriv = jnp.asarray(derivative_table(), jnp.float32)
    weights = point_weights()
    lam_wide = lam_cells.astype(jnp.float32)[:, None, :, None, :, None, None]
    mu_wide = mu_cells.astype(jnp.float32)[:, None, :, None, :, None, None]
    primal_grad = gradients(to_cells(primal_nodes).astype(jnp.float32), deriv)
    primal_force = internal_forces(primal_grad, lam_wide, mu_wide, deriv, weights, 1)
    sensitivity = internal_forces(primal_grad, 0.0, 1.0, deriv, weights, 1)
    tangent_grad = gradients(to_cells(tangent_nodes).astype(jnp.float32), deriv)
    directions = select.shape[-1]
    tangent_force = internal_forces(tangent_grad, lam_wide, mu_wide, deriv, weights, directions)
    source = sensitivity[..., :, None] * select.astype(jnp.float32)[:, None, :, None, :, None, None, :]
    tangent_force = tangent_force + source.reshape(tangent_force.shape)
    return to_nodes(primal_force), to_nodes(tangent_force)


def reference(disp, disp_prev, tangent, tangent_prev, lame_lambda, lame_mu, node_mass, force, cell_block, direction_block, port_id, port_mode):
    directions = direction_block.shape[0]
    node_shape = disp.shape[:3] + (3 * directions,)
    tangent = tangent.reshape(node_shape)
    tangent_prev = tangent_prev.reshape(node_shape)
    padding = ((0, 1), (0, 1), (0, 0), (0, 0))
    padded_disp = jnp.pad(disp, padding)
    padded_tangent = jnp.pad(tangent, padding)
    select = (cell_block[..., None] == direction_block[None, None, None, :]).astype(jnp.float32)

    def one_layer(layer_index, sums):
        primal_acc, tangent_acc = sums
        layer_at = jnp.asarray(layer_index).astype(jnp.int32)
        start = (layer_at * 5).astype(jnp.int32)
        node_disp = lax.dynamic_slice_in_dim(padded_disp, start, 6, 0)
        node_tangent = lax.dynamic_slice_in_dim(padded_tangent, start, 6, 0)
        lam_layer = lax.dynamic_slice_in_dim(lame_lambda, layer_at, 1, 0)
        mu_layer = lax.dynamic_slice_in_dim(lame_mu, layer_at, 1, 0)
        select_layer = lax.dynamic_slice_in_dim(select, layer_at, 1, 0)
        primal_part, tangent_part = block_forces(node_disp, node_tangent, lam_layer, mu_layer, select_layer)
        primal_acc = lax.dynamic_update_slice_in_dim(primal_acc, lax.dynamic_slice_in_dim(primal_acc, start, 6, 0) + primal_part, start, 0)
        tangent_acc = lax.dynamic_update_slice_in_dim(tangent_acc, lax.dynamic_slice_in_dim(tangent_acc, start, 6, 0) + tangent_part, start, 0)
        return primal_acc, tangent_acc

    initial = (jnp.zeros(padded_disp.shape, jnp.float32), jnp.zeros(padded_tangent.shape, jnp.float32))
    primal_acc, tangent_acc = lax.fori_loop(0, lame_lambda.shape[0], one_layer, initial)
    primal_force = primal_acc[:disp.shape[0], :disp.shape[1]]
    tangent_force = tangent_acc[:disp.shape[0], :disp.shape[1]]
    mass = node_mass[..., None]
    disp_next = (2.0 * disp.astype(jnp.float32) - disp_prev.astype(jnp.float32) + STEP_SQUARED * (force.astype(jnp.float32) - primal_force) / mass).astype(jnp.bfloat16)
    tangent_full = 2.0 * tangent.astype(jnp.float32) - tangent_prev.astype(jnp.float32) - STEP_SQUARED * tangent_force / mass
    modes = port_mode.astype(jnp.float32)
    weighted = modes[..., 0:1] * tangent_full[..., 0:directions]
    weighted = weighted + modes[..., 1:2] * tangent_full[..., directions:2 * directions]
    weighted = weighted + modes[..., 2:3] * tangent_full[..., 2 * directions:3 * directions]
    port_amp = jax.ops.segment_sum(weighted.reshape(-1, directions), port_id.reshape(-1), num_segments=PORTS + 1)[:PORTS]
    tangent_next = tangent_full.astype(jnp.bfloat16).reshape(disp.shape[0], disp.shape[1], -1)
    return disp_next, tangent_next, port_amp
```

```python
import functools

import jax
import jax.numpy as jnp
import numpy as np
from jax import lax
from jax.experimental import pallas as pl
from jax.experimental.pallas import tpu as pltpu
from jax.sharding import PartitionSpec as P

PORTS = 64
PORT_DEPTH = 40
EZ = 5
NT = 64
NZN = 26
GLL_POINTS = np.array(
    [-1.0, -0.765055323929465, -0.285231516480645, 0.285231516480645, 0.765055323929465, 1.0]
)
GLL_WEIGHTS = np.array(
    [
        1.0 / 15.0,
        0.378474956297847,
        0.554858377035486,
        0.554858377035486,
        0.378474956297847,
        1.0 / 15.0,
    ]
)
STEP_SQUARED = 0.03
MESH = pl.DeviceIdType.MESH
F32 = jnp.float32
BF16 = jnp.bfloat16
COLS = 3 * NZN * NT
WIDE = COLS + 128
SPLITS = 2
PAIRS = ((0, 1), (2, 3), (5, 6), (7, 8), (4, 9))


def derivative_table():
    identity = np.eye(6)
    differences = GLL_POINTS[:, None] - GLL_POINTS[None, :] + identity
    barycentric = 1.0 / np.prod(differences, axis=1)
    matrix = barycentric[None, :] / barycentric[:, None] / differences
    matrix = matrix * (1.0 - identity)
    matrix = matrix - identity * matrix.sum(axis=1)[:, None]
    return matrix


def split_bf16(table):
    high = table.astype(jnp.bfloat16)
    low = (table - high.astype(np.float64)).astype(jnp.bfloat16)
    return [high, low]


def element_tables():
    d = derivative_table()
    eye = np.eye(6)
    ds = [
        np.kron(np.kron(d, eye), eye),
        np.kron(np.kron(eye, d), eye),
        np.kron(np.kron(eye, eye), d),
    ]
    w = np.kron(np.kron(GLL_WEIGHTS, GLL_WEIGHTS), GLL_WEIGHTS)[:, None]
    lap = sum(m.T @ (w * m) for m in ds)
    both = np.zeros((2, 216, 3, 216, 3))
    for c in range(3):
        for e in range(3):
            both[0, :, c, :, e] = ds[c].T @ (w * ds[e])
            both[1, :, c, :, e] = ds[e].T @ (w * ds[c]) + (lap if c == e else 0.0)
    both = both.reshape(2, 6, 6, 6, 3, 6, 6, 6, 3)
    both = both.transpose(0, 1, 3, 4, 2, 5, 7, 8, 6)
    pad = [(0, 0)] * 9
    pad[4] = (0, 2)
    pad[8] = (0, 2)
    both = np.pad(both, pad).reshape(2, 6, 144, 864)
    both = both.transpose(1, 0, 2, 3).reshape(6, 288, 864)
    return np.stack(split_bf16(both)[:SPLITS])


def layout_tables():
    expand = np.zeros((128, NZN, 3, NT))
    for k in range(NZN):
        for c in range(3):
            expand[c * 32 + k, k, c, :] = 1.0
    gather = np.zeros((2, 128, 18, 128))
    for ey in range(2):
        for ez in range(EZ):
            for kz in range(6):
                for c in range(3):
                    gather[ey, c * 32 + 5 * ez + kz, kz * 3 + c, ey * 5 + ez] = 1.0
    gather = gather.reshape(256, 18 * 128)
    return (
        expand.reshape(128, COLS).astype(jnp.bfloat16),
        gather.astype(jnp.bfloat16),
        np.ascontiguousarray(gather.T).astype(jnp.bfloat16),
    )


def lane_tile(t):
    return slice(t * 128, (t + 1) * 128)


def hi_lo(values):
    high = values.astype(BF16)
    return high, (values - high.astype(F32)).astype(BF16)


def dot(a, b):
    return jnp.dot(a, b, preferred_element_type=F32)


def kernel(
    nx, ny, nsrc_y,
    lame, cells, dirs, tan, tanp, prep, mass, pid, k_hbm, e_hbm, p_hbm, q_hbm,
    tan_out, disp_out, port_out,
    kv, ev, pv, qv, const_sem,
    txf, tpf, exf, wf, oh, uh, ul, ms, ps, dsc, z, o, fs, fpb,
    s1x, s1y, s1d, r1x, r1y, r1d, s2x, s2y, s2d, r2x, r2y, r2d,
    pbuf, prec, send_sem, recv_sem, psend, precv,
):
    gx = lax.axis_index("gx")
    gy = lax.axis_index("gy")
    consts = [
        pltpu.make_async_copy(a, b, const_sem.at[i])
        for i, (a, b) in enumerate(((e_hbm, ev), (p_hbm, pv), (k_hbm, kv), (q_hbm, qv)))
    ]
    for copy in consts:
        copy.start()

    x_lo, x_hi = gx > 0, gx < nx - 1
    y_lo, y_hi = gy > 0, gy < ny - 1
    first_src = ny - nsrc_y
    is_src = gy >= first_src
    n_all = nx * ny
    me = gx * ny + gy

    barrier = pltpu.get_barrier_semaphore()
    around = (
        (x_lo, -1, 0), (x_hi, 1, 0), (y_lo, 0, -1), (y_hi, 0, 1),
        (jnp.logical_and(x_lo, y_lo), -1, -1), (jnp.logical_and(x_hi, y_hi), 1, 1),
    )
    expected = jnp.int32(0)
    for there, dx, dy in around:
        @pl.when(there)
        def _(dx=dx, dy=dy):
            pl.semaphore_signal(barrier, inc=1, device_id=(gx + dx, gy + dy), device_id_type=MESH)
        expected = expected + there.astype(jnp.int32)

    def greet(s, carry):
        sx = s // nsrc_y
        sy = first_src + s % nsrc_y

        @pl.when(sx * ny + sy != me)
        def _():
            pl.semaphore_signal(barrier, inc=1, device_id=(sx, sy), device_id_type=MESH)
        return carry

    lax.fori_loop(0, nx * nsrc_y, greet, 0)
    expected = expected + is_src.astype(jnp.int32) * (n_all - 1)

    s1x[...] = jnp.zeros_like(s1x)
    s1y[...] = jnp.zeros_like(s1y)
    s1d[...] = jnp.zeros_like(s1d)
    s1x[0:10, 0:COLS] = tan[0]
    s1x[:, COLS:] = prep[0, 0]
    for x in range(5):
        s1y[x:x + 1, 0:COLS] = tan[x, 0:1, :]
        s1y[x:x + 1, COLS:] = prep[0, x, 0:1, :]
    row = jnp.concatenate([tan[0, 0:1, :], prep[0, 0, 0:1, :]], axis=1)
    for r in range(14):
        width = min(384, WIDE - r * 384)
        s1d[r:r + 1, 0:width] = row[:, r * 384:r * 384 + width]

    pl.semaphore_wait(barrier, expected)

    def remote(index, src, dst, dx, dy):
        return pltpu.make_async_remote_copy(
            src_ref=src, dst_ref=dst, send_sem=send_sem.at[index], recv_sem=recv_sem.at[index],
            device_id=(gx + dx, gy + dy), device_id_type=MESH,
        )

    first = (
        (remote(0, s1x, r1x, -1, 0), x_lo, x_hi, r1x),
        (remote(1, s1y, r1y, 0, -1), y_lo, y_hi, r1y),
        (remote(2, s1d, r1d, -1, -1), jnp.logical_and(x_lo, y_lo), jnp.logical_and(x_hi, y_hi), r1d),
    )
    second = (
        (remote(3, s2x, r2x, 1, 0), x_hi, x_lo, r2x),
        (remote(4, s2y, r2y, 0, 1), y_hi, y_lo, r2y),
        (remote(5, s2d, r2d, 1, 1), jnp.logical_and(x_hi, y_hi), jnp.logical_and(x_lo, y_lo), r2d),
    )

    def start(item):
        copy, sends, _, _ = item

        @pl.when(sends)
        def _():
            copy.start()

    def arrived(item):
        copy, _, receives, buffer = item

        @pl.when(receives)
        def _():
            copy.wait_recv()

        @pl.when(jnp.logical_not(receives))
        def _():
            buffer[...] = jnp.zeros_like(buffer)

    def sent(item):
        copy, sends, _, _ = item

        @pl.when(sends)
        def _():
            copy.wait_send()

    for item in first:
        start(item)

    lane = lax.broadcasted_iota(jnp.int32, (1, 128), 1)
    low_half = lane < 64

    def halves(a, b):
        return jnp.where(low_half, a, b)

    def prepare(x, carry):
        txf[x, 8:16, :] = jnp.zeros((8, WIDE), F32)
        tpf[x, 8:16, :] = jnp.zeros((8, COLS), F32)
        txf[x, 0:10, 0:COLS] = tan[x].astype(F32)
        txf[x, :, COLS:] = prep[0, x].astype(F32)
        tpf[x, 0:10, :] = tanp[x].astype(F32)
        ms[...] = jnp.ones_like(ms)
        ps[...] = jnp.full(ps.shape, PORTS, jnp.int32)
        ms[0:10, 0:NZN] = mass[x]
        ps[0:10, 0:NZN] = pid[x]
        rep_row = lax.broadcasted_iota(jnp.int32, (128, 128), 0)
        rep_col = lax.broadcasted_iota(jnp.int32, (128, 128), 1)
        rep = jnp.where((rep_col % 32 == rep_row) & (rep_row < NZN), 1.0, 0.0).astype(BF16)
        inv_hi, inv_lo = hi_lo(STEP_SQUARED / ms[...])
        exf[x, 0:16] = dot(inv_hi, rep).astype(BF16)
        exf[x, 16:32] = dot(inv_lo, rep).astype(BF16)
        exf[x, 32:48] = prep[3, x]
        ids = ps[...]
        rows = pl.ds(pl.multiple_of(x * 16, 16), 16)
        for pair in range(13):
            port = halves(ids[:, 2 * pair:2 * pair + 1], ids[:, 2 * pair + 1:2 * pair + 2])
            oh[pair, rows, :] = jnp.where(port == lane % 64, 1.0, 0.0).astype(BF16)
        return carry

    lax.fori_loop(0, 5, prepare, 0)

    consts[0].wait()
    lhs = exf[...].reshape(240, 128)

    def widen(n, carry):
        cols = pl.ds(pl.multiple_of(n * 384, 384), 384)
        w = dot(lhs, ev[:, cols]).reshape(5, 48, 384)
        wf[:, 0:16, cols] = w[:, 0:16] + w[:, 16:32]
        wf[:, 16:32, cols] = w[:, 32:48]
        return carry

    lax.fori_loop(0, COLS // 384, widen, 0)

    for item in first:
        arrived(item)
    for x in range(5):
        txf[x, 10:11, :] = r1y[x:x + 1, :].astype(F32)
    txf[5] = r1x[...].astype(F32)
    for r in range(14):
        width = min(384, WIDE - r * 384)
        txf[5, 10:11, r * 384:r * 384 + width] = r1d[r:r + 1, 0:width].astype(F32)

    consts[1].wait()
    near = jnp.concatenate([txf[x, 0:8, COLS:] for x in range(6)], axis=0)
    far = jnp.concatenate([txf[x, 5:13, COLS:] for x in range(6)], axis=0)
    gathered = dot(jnp.concatenate([near, far], axis=1).astype(BF16), pv[...])
    dsc[...] = gathered.reshape(6, 8, 18 * 128)

    def fill(x, carry):
        def tile(m, ey, ez):
            kc = 15 * ez + m
            return txf[x, 5 * ey:5 * ey + 8, lane_tile(kc // 2)]

        for mp in range(9):
            for i, (e1, e2) in enumerate(PAIRS):
                both = []
                for m in (2 * mp, 2 * mp + 1):
                    a, b = tile(m, e1 // 5, e1 % 5), tile(m, e2 // 5, e2 % 5)
                    a_half, b_half = (15 * (e1 % 5) + m) % 2, (15 * (e2 % 5) + m) % 2
                    if a_half == 0 and b_half == 1:
                        both.append(halves(a, b))
                    elif a_half == 1 and b_half == 0:
                        both.append(pltpu.roll(halves(b, a), 64, 1))
                    elif a_half == 0:
                        both.append(halves(a, pltpu.roll(b, 64, 1)))
                    else:
                        both.append(halves(pltpu.roll(a, 64, 1), b))
                z[x, 16 * mp:16 * mp + 16, lane_tile(i)] = jnp.concatenate(both, axis=0).astype(BF16)
            both = [dsc[x, :, lane_tile(2 * mp)], dsc[x, :, lane_tile(2 * mp + 1)]]
            z[x, 16 * mp:16 * mp + 16, lane_tile(5)] = jnp.concatenate(both, axis=0).astype(BF16)
        return carry

    lax.fori_loop(0, 6, fill, 0)
    consts[2].wait()

    def apply_far(n, carry):
        cols = pl.ds(pl.multiple_of(n * 256, 256), 256)
        rhs = z[:, :, cols].reshape(864, 256)
        o[5, :, cols] = sum(dot(kv[s, 5], rhs) for s in range(SPLITS))
        return carry

    def apply_near(n, carry):
        cols = pl.ds(pl.multiple_of(n * 256, 256), 256)
        rhs = z[:, :, cols].reshape(864, 256)
        for x in range(0, 5):
            o[x, :, cols] = sum(dot(kv[s, x], rhs) for s in range(SPLITS))
        return carry

    lam_rows = [halves(lame[a], lame[b]) for a, b in PAIRS]
    mu_rows = [halves(lame[10 + a], lame[10 + b]) for a, b in PAIRS]
    lam_point = sum(jnp.where(lane == e, lame[e], 0.0) for e in range(10))
    mu_point = sum(jnp.where(lane == e, lame[10 + e], 0.0) for e in range(10))
    sel_row = lax.broadcasted_iota(jnp.int32, (128, 128), 0)
    direction = dirs[...]
    choose = jnp.concatenate(
        [
            jnp.where(
                (sel_row == halves(a, b)) & (direction == halves(cells[a], cells[b])), 1.0, 0.0
            ).astype(BF16)
            for a, b in PAIRS
        ],
        axis=1,
    )

    def assemble(x):
        tile5 = o[x, 144:288, lane_tile(5)]
        point = lam_point * o[x, 0:144, lane_tile(5)] + mu_point * tile5
        point = jnp.concatenate([point[8 * m:8 * m + 8] for m in range(18)], axis=1)
        point_hi = point.astype(BF16).astype(F32)
        fpb[x] = jnp.concatenate([point_hi, point - point_hi], axis=0).astype(BF16)
        k_hi, k_lo = hi_lo(tile5)
        source = dot(k_hi, choose) + dot(k_lo, choose)
        force = [
            lam_rows[i] * o[x, 0:144, lane_tile(i)]
            + mu_rows[i] * o[x, 144:288, lane_tile(i)]
            + source[:, lane_tile(i)]
            for i in range(5)
        ]
        fs[x, 8:16, :] = jnp.zeros((8, WIDE), F32)
        for ey in range(2):
            for t in range(39):
                stay, move = ([], []), ([], [])
                for h in range(2):
                    kc = 2 * t + h
                    ez, m = kc // 15, kc % 15
                    for ez_at, m_at in ((ez, m), (ez - 1, m + 15)):
                        if 0 <= ez_at < EZ and m_at < 18:
                            e = ey * 5 + ez_at
                            i = next(n for n, p in enumerate(PAIRS) if e in p)
                            half = PAIRS[i].index(e)
                            piece = force[i][8 * m_at:8 * m_at + 8]
                            (stay if half == h else move)[half].append(piece)
                zero = jnp.zeros((8, 128), F32)
                total = halves(sum(stay[0], zero), sum(stay[1], zero))
                if move[0] or move[1]:
                    total = total + pltpu.roll(
                        halves(sum(move[0], zero), sum(move[1], zero)), 64, 1
                    )
                if ey == 0:
                    fs[x, 0:8, lane_tile(t)] = total
                else:
                    fs[x, 5:13, lane_tile(t)] = fs[x, 5:13, lane_tile(t)] + total

    def place_point(x, values):
        values = values[0:8] + values[8:16]
        fs[x, 0:8, COLS:] = values[:, 0:128]
        fs[x, 5:13, COLS:] = fs[x, 5:13, COLS:] + values[:, 128:256]

    lax.fori_loop(0, 3, apply_far, 0)
    assemble(5)
    consts[3].wait()
    place_point(5, dot(fpb[5], qv[...]))
    s2x[...] = fs[5].astype(BF16)
    s2d[...] = jnp.zeros_like(s2d)
    corner = fs[5, 10:11, :].astype(BF16)
    for r in range(14):
        width = min(384, WIDE - r * 384)
        s2d[r:r + 1, 0:width] = corner[:, r * 384:r * 384 + width]
    start(second[0])
    start(second[2])

    lax.fori_loop(0, 3, apply_near, 0)

    def assemble_near(x, carry):
        assemble(x)
        return carry

    lax.fori_loop(0, 5, assemble_near, 0)
    points = dot(fpb[0:5].reshape(80, 18 * 128), qv[...])
    s2y[...] = jnp.zeros_like(s2y)
    for x in range(5):
        place_point(x, points[16 * x:16 * x + 16])
        s2y[x:x + 1, :] = fs[x, 10:11, :].astype(BF16)
    start(second[1])

    for item in second:
        arrived(item)
    fs[0] = fs[0] + r2x[...].astype(F32)
    for x in range(5):
        fs[x, 0:1, :] = fs[x, 0:1, :] + r2y[x:x + 1, :].astype(F32)
    for r in range(14):
        width = min(384, WIDE - r * 384)
        cols = slice(r * 384, r * 384 + width)
        fs[0, 0:1, cols] = fs[0, 0:1, cols] + r2d[r:r + 1, 0:width].astype(F32)

    def finish(x, carry):
        scale = exf[x, 0:16].astype(F32) + exf[x, 16:32].astype(F32)
        moved = (
            2.0 * txf[x, :, COLS:]
            - prep[1, x].astype(F32)
            + scale * (prep[2, x].astype(F32) - fs[x, :, COLS:])
        )
        disp_out[x] = moved.astype(BF16)
        rows = pl.ds(pl.multiple_of(x * 16, 16), 16)
        for pair in range(13):
            parts = []
            for t in range(3 * pair, 3 * pair + 3):
                cols = lane_tile(t)
                full = 2.0 * txf[x, :, cols] - tpf[x, :, cols] - wf[x, 0:16, cols] * fs[x, :, cols]
                tan_out[x, :, cols] = full[0:10].astype(BF16)
                parts.append(full * wf[x, 16:32, cols])
            a, b, c = parts
            amount = halves(a + pltpu.roll(a, 64, 1), c + pltpu.roll(c, 64, 1)) + b
            high, low = hi_lo(amount)
            uh[pair, rows, :] = high
            ul[pair, rows, :] = low
        return carry

    lax.fori_loop(0, 5, finish, 0)

    per_row = PORTS // ny
    slot = gx * nsrc_y + (gy - first_src)

    def port_copy(target_x, target_y, slot_at):
        return pltpu.make_async_remote_copy(
            src_ref=pbuf.at[target_y], dst_ref=prec.at[slot_at],
            send_sem=psend.at[target_x * ny + target_y], recv_sem=precv.at[slot_at],
            device_id=(target_x, target_y), device_id_type=MESH,
        )

    @pl.when(is_src)
    def _():
        onehot = oh[...].reshape(1040, 128)
        dims = (((0,), (0,)), ((), ()))
        square = lax.dot_general(
            onehot, uh[...].reshape(1040, 128), dims, preferred_element_type=F32
        ) + lax.dot_general(onehot, ul[...].reshape(1040, 128), dims, preferred_element_type=F32)
        amp = square[0:64] + pltpu.roll(square[64:128], 64, 1)
        for g in range(ny):
            pbuf[g] = jnp.zeros((8, 128), F32)
            pbuf[g, 0:per_row, :] = amp[g * per_row:(g + 1) * per_row]

        def send(t, carry):
            @pl.when(t != me)
            def _():
                port_copy(t // ny, t % ny, slot).start()
            return carry

        lax.fori_loop(0, n_all, send, 0)
        prec[slot] = pbuf[gy]

    def collect(s, acc):
        @pl.when(jnp.logical_or(jnp.logical_not(is_src), s != slot))
        def _():
            port_copy(gx, gy, s).wait_recv()
        return acc + prec[s]

    acc = lax.fori_loop(0, nx * nsrc_y, collect, jnp.zeros((8, 128), F32))
    per_col = NT // nx
    mine = acc[0:per_row, 0:per_col]
    for h in range(1, nx):
        mine = jnp.where(gx == h, acc[0:per_row, h * per_col:(h + 1) * per_col], mine)
    port_out[...] = mine

    for item in first + second:
        sent(item)

    @pl.when(is_src)
    def _():
        def drain(t, carry):
            @pl.when(t != me)
            def _():
                port_copy(t // ny, t % ny, slot).wait_send()
            return carry

        lax.fori_loop(0, n_all, drain, 0)


def per_device(
    nx, ny,
    disp, disp_prev, tangent, tangent_prev, lame_lambda, lame_mu, node_mass, force,
    cell_block, direction_block, port_id, port_mode,
):
    rows = disp.shape[1]
    nsrc_y = -(-PORT_DEPTH // rows)
    lame = jnp.concatenate([lame_lambda.reshape(-1), lame_mu.reshape(-1)]).astype(F32)
    dirs = jnp.concatenate([direction_block, direction_block])[None]
    stacked = jnp.stack([disp, disp_prev, force, port_mode]).transpose(0, 1, 2, 4, 3)
    stacked = jnp.pad(stacked, ((0, 0), (0, 0), (0, 16 - rows), (0, 1), (0, 32 - NZN)))
    prep = stacked.reshape(4, 5, 16, 128)
    expand, gather, scatter = layout_tables()
    tables = element_tables()
    nsrc = nx * nsrc_y
    vmem = pl.BlockSpec(memory_space=pltpu.VMEM)
    smem = pl.BlockSpec(memory_space=pltpu.SMEM)
    hbm = pl.BlockSpec(memory_space=pl.ANY)
    big = pltpu.VMEM((16, WIDE), BF16)
    small = pltpu.VMEM((16, 384), BF16)
    tangent_next, moved, port_amp = pl.pallas_call(
        functools.partial(kernel, nx, ny, nsrc_y),
        out_shape=(
            jax.ShapeDtypeStruct(tangent.shape, BF16),
            jax.ShapeDtypeStruct((5, 16, 128), BF16),
            jax.ShapeDtypeStruct((PORTS // ny, NT // nx), F32),
        ),
        in_specs=[smem, smem] + [vmem] * 6 + [hbm] * 4,
        out_specs=(vmem, vmem, vmem),
        scratch_shapes=[
            pltpu.VMEM(tables.shape, BF16),
            pltpu.VMEM(expand.shape, BF16),
            pltpu.VMEM(gather.shape, BF16),
            pltpu.VMEM(scatter.shape, BF16),
            pltpu.SemaphoreType.DMA((4,)),
            pltpu.VMEM((6, 16, WIDE), F32),
            pltpu.VMEM((5, 16, COLS), F32),
            pltpu.VMEM((5, 48, 128), BF16),
            pltpu.VMEM((5, 32, COLS), F32),
            pltpu.VMEM((13, 80, 128), BF16),
            pltpu.VMEM((13, 80, 128), BF16),
            pltpu.VMEM((13, 80, 128), BF16),
            pltpu.VMEM((16, 128), F32),
            pltpu.VMEM((16, 128), jnp.int32),
            pltpu.VMEM((6, 8, 18 * 128), F32),
            pltpu.VMEM((6, 144, 768), BF16),
            pltpu.VMEM((6, 288, 768), F32),
            pltpu.VMEM((6, 16, WIDE), F32),
            pltpu.VMEM((6, 16, 18 * 128), BF16),
            big, big, small, big, big, small,
            big, big, small, big, big, small,
            pltpu.VMEM((ny, 8, 128), F32),
            pltpu.VMEM((nsrc, 8, 128), F32),
            pltpu.SemaphoreType.DMA((6,)),
            pltpu.SemaphoreType.DMA((6,)),
            pltpu.SemaphoreType.DMA((nx * ny,)),
            pltpu.SemaphoreType.DMA((nsrc,)),
        ],
        compiler_params=pltpu.CompilerParams(
            collective_id=0, has_side_effects=True, vmem_limit_bytes=56 * 1024 * 1024
        ),
    )(
        lame, cell_block.reshape(-1), dirs, tangent, tangent_prev, prep, node_mass, port_id,
        jnp.asarray(tables), jnp.asarray(expand), jnp.asarray(gather), jnp.asarray(scatter),
    )
    moved = moved.reshape(5, 16, 4, 32)[:, :rows, :3, :NZN].transpose(0, 1, 3, 2)
    return moved, tangent_next, port_amp


def solution(mesh):
    nx, ny = mesh.shape["gx"], mesh.shape["gy"]
    return jax.shard_map(
        functools.partial(per_device, nx, ny),
        mesh=mesh,
        in_specs=(
            P("gx", "gy", None, None),
            P("gx", "gy", None, None),
            P("gx", "gy", None),
            P("gx", "gy", None),
            P("gx", "gy", None),
            P("gx", "gy", None),
            P("gx", "gy", None),
            P("gx", "gy", None, None),
            P("gx", "gy", None),
            P(),
            P("gx", "gy", None),
            P("gx", "gy", None, None),
        ),
        out_specs=(P("gx", "gy", None, None), P("gx", "gy", None), P("gy", "gx")),
        check_vma=False,
    )
```

```python
import functools

import jax
import jax.numpy as jnp
import numpy as np
from jax import lax
from jax.experimental import pallas as pl
from jax.experimental.pallas import tpu as pltpu
from jax.sharding import PartitionSpec as P

PORTS = 64
PORT_DEPTH = 40
EZ = 5
NT = 64
NZN = 26
GLL_POINTS = np.array(
    [-1.0, -0.765055323929465, -0.285231516480645, 0.285231516480645, 0.765055323929465, 1.0]
)
GLL_WEIGHTS = np.array(
    [
        1.0 / 15.0,
        0.378474956297847,
        0.554858377035486,
        0.554858377035486,
        0.378474956297847,
        1.0 / 15.0,
    ]
)
STEP_SQUARED = 0.03
MESH = pl.DeviceIdType.MESH
F32 = jnp.float32
BF16 = jnp.bfloat16
COLS = 3 * NZN * NT
WIDE = COLS + 128
SPLITS = 2
PAIRS = ((0, 1), (2, 3), (5, 6), (7, 8), (4, 9))


def derivative_table():
    identity = np.eye(6)
    differences = GLL_POINTS[:, None] - GLL_POINTS[None, :] + identity
    barycentric = 1.0 / np.prod(differences, axis=1)
    matrix = barycentric[None, :] / barycentric[:, None] / differences
    matrix = matrix * (1.0 - identity)
    matrix = matrix - identity * matrix.sum(axis=1)[:, None]
    return matrix


def split_bf16(table):
    high = table.astype(jnp.bfloat16)
    low = (table - high.astype(np.float64)).astype(jnp.bfloat16)
    return [high, low]


def element_tables():
    d = derivative_table()
    eye = np.eye(6)
    ds = [
        np.kron(np.kron(d, eye), eye),
        np.kron(np.kron(eye, d), eye),
        np.kron(np.kron(eye, eye), d),
    ]
    w = np.kron(np.kron(GLL_WEIGHTS, GLL_WEIGHTS), GLL_WEIGHTS)[:, None]
    lap = sum(m.T @ (w * m) for m in ds)
    both = np.zeros((2, 216, 3, 216, 3))
    for c in range(3):
        for e in range(3):
            both[0, :, c, :, e] = ds[c].T @ (w * ds[e])
            both[1, :, c, :, e] = ds[e].T @ (w * ds[c]) + (lap if c == e else 0.0)
    both = both.reshape(2, 6, 6, 6, 3, 6, 6, 6, 3)
    both = both.transpose(0, 1, 3, 4, 2, 5, 7, 8, 6)
    pad = [(0, 0)] * 9
    pad[4] = (0, 2)
    pad[8] = (0, 2)
    both = np.pad(both, pad).reshape(2, 6, 144, 864)
    both = both.transpose(1, 0, 2, 3).reshape(6, 288, 864)
    return np.stack(split_bf16(both)[:SPLITS])


def layout_tables():
    expand = np.zeros((128, NZN, 3, NT))
    for k in range(NZN):
        for c in range(3):
            expand[c * 32 + k, k, c, :] = 1.0
    gather = np.zeros((2, 128, 18, 128))
    for ey in range(2):
        for ez in range(EZ):
            for kz in range(6):
                for c in range(3):
                    gather[ey, c * 32 + 5 * ez + kz, kz * 3 + c, ey * 5 + ez] = 1.0
    gather = gather.reshape(256, 18 * 128)
    return (
        expand.reshape(128, COLS).astype(jnp.bfloat16),
        gather.astype(jnp.bfloat16),
        np.ascontiguousarray(gather.T).astype(jnp.bfloat16),
    )


X_PACK = (
    (np.s_[0:10, 0:3200], np.s_[0:10, 0:3200]),
    (np.s_[10:16, 0:1920], np.s_[0:6, 3200:5120]),
    (np.s_[10:14, 1920:3200], np.s_[6:10, 3200:4480]),
    (np.s_[14:16, 1920:2560], np.s_[6:8, 4480:5120]),
    (np.s_[14:16, 2560:3200], np.s_[8:10, 4480:5120]),
)


def lane_tile(t):
    return slice(t * 128, (t + 1) * 128)


def hi_lo(values):
    high = values.astype(BF16)
    return high, (values - high.astype(F32)).astype(BF16)


def dot(a, b):
    return jnp.dot(a, b, preferred_element_type=F32)


def kernel(
    nx, ny, nsrc_y,
    lam_ref, mu_ref, cell_ref, dir_ref, tan, tanp, prep, mass, pid, k_hbm, e_hbm, p_hbm, q_hbm,
    tan_out, disp_out, port_out,
    kv, ev, pv, qv, const_sem,
    txf, tpf, exf, wf, oh, uh, ul, ms, ps, dsc, z, o, fs, fpb,
    s1x, s1y, s1d, r1x, r1y, r1d, s2x, s2y, s2d, s2p, r2x, r2y, r2d, r2p,
    pbuf, prec, send_sem, recv_sem, psend, precv,
):
    gx = lax.axis_index("gx")
    gy = lax.axis_index("gy")
    consts = [
        pltpu.make_async_copy(a, b, const_sem.at[i])
        for i, (a, b) in enumerate(((e_hbm, ev), (p_hbm, pv), (k_hbm, kv), (q_hbm, qv)))
    ]
    for copy in consts:
        copy.start()

    x_lo, x_hi = gx > 0, gx < nx - 1
    y_lo, y_hi = gy > 0, gy < ny - 1
    first_src = ny - nsrc_y
    is_src = gy >= first_src
    n_all = nx * ny
    me = gx * ny + gy

    barrier = pltpu.get_barrier_semaphore()
    around = (
        (x_lo, -1, 0), (x_hi, 1, 0), (y_lo, 0, -1), (y_hi, 0, 1),
        (jnp.logical_and(x_lo, y_lo), -1, -1), (jnp.logical_and(x_hi, y_hi), 1, 1),
    )
    expected = jnp.int32(0)
    for there, dx, dy in around:
        @pl.when(there)
        def _(dx=dx, dy=dy):
            pl.semaphore_signal(barrier, inc=1, device_id=(gx + dx, gy + dy), device_id_type=MESH)
        expected = expected + there.astype(jnp.int32)

    def greet(s, carry):
        sx = s // nsrc_y
        sy = first_src + s % nsrc_y

        @pl.when(sx * ny + sy != me)
        def _():
            pl.semaphore_signal(barrier, inc=1, device_id=(sx, sy), device_id_type=MESH)
        return carry

    lax.fori_loop(0, nx * nsrc_y, greet, 0)
    expected = expected + is_src.astype(jnp.int32) * (n_all - 1)

    s1y[...] = jnp.zeros_like(s1y)
    s1d[...] = jnp.zeros_like(s1d)
    layer = jnp.concatenate([tan[0], prep[0, 0, 0:10, :]], axis=1)
    for to, at in X_PACK:
        s1x[to] = layer[at]
    for x in range(5):
        s1y[x:x + 1, 0:COLS] = tan[x, 0:1, :]
        s1y[x:x + 1, COLS:] = prep[0, x, 0:1, :]
    row = jnp.concatenate([tan[0, 0:1, :], prep[0, 0, 0:1, :]], axis=1)
    for r in range(14):
        width = min(384, WIDE - r * 384)
        s1d[r:r + 1, 0:width] = row[:, r * 384:r * 384 + width]

    pl.semaphore_wait(barrier, expected)

    def remote(index, src, dst, dx, dy):
        return pltpu.make_async_remote_copy(
            src_ref=src, dst_ref=dst, send_sem=send_sem.at[index], recv_sem=recv_sem.at[index],
            device_id=(gx + dx, gy + dy), device_id_type=MESH,
        )

    first = (
        (remote(0, s1x, r1x, -1, 0), x_lo, x_hi, r1x),
        (remote(1, s1y, r1y, 0, -1), y_lo, y_hi, r1y),
        (remote(2, s1d, r1d, -1, -1), jnp.logical_and(x_lo, y_lo), jnp.logical_and(x_hi, y_hi), r1d),
    )
    second = (
        (remote(3, s2x, r2x, 1, 0), x_hi, x_lo, r2x),
        (remote(4, s2d, r2d, 1, 1), jnp.logical_and(x_hi, y_hi), jnp.logical_and(x_lo, y_lo), r2d),
        (remote(5, s2p, r2p, 0, 1), y_hi, y_lo, r2p),
    ) + tuple(
        (remote(6 + x, s2y.at[x], r2y.at[x], 0, 1), y_hi, y_lo, r2y.at[x]) for x in range(5)
    )

    def start(item):
        copy, sends, _, _ = item

        @pl.when(sends)
        def _():
            copy.start()

    def arrived(item):
        copy, _, receives, buffer = item

        @pl.when(receives)
        def _():
            copy.wait_recv()

        @pl.when(jnp.logical_not(receives))
        def _():
            buffer[...] = jnp.zeros_like(buffer)

    def sent(item):
        copy, sends, _, _ = item

        @pl.when(sends)
        def _():
            copy.wait_send()

    for item in first:
        start(item)

    lane = lax.broadcasted_iota(jnp.int32, (1, 128), 1)
    low_half = lane < 64

    def halves(a, b):
        return jnp.where(low_half, a, b)

    def prepare(x, carry):
        txf[x, 8:16, :] = jnp.zeros((8, WIDE), F32)
        tpf[x, 8:16, :] = jnp.zeros((8, COLS), F32)
        txf[x, 0:10, 0:COLS] = tan[x].astype(F32)
        txf[x, :, COLS:] = prep[0, x].astype(F32)
        tpf[x, 0:10, :] = tanp[x].astype(F32)
        ms[...] = jnp.ones_like(ms)
        ps[...] = jnp.full(ps.shape, PORTS, jnp.int32)
        ms[0:10, 0:NZN] = mass[x]
        ps[0:10, 0:NZN] = pid[x]
        rep_row = lax.broadcasted_iota(jnp.int32, (128, 128), 0)
        rep_col = lax.broadcasted_iota(jnp.int32, (128, 128), 1)
        rep = jnp.where((rep_col % 32 == rep_row) & (rep_row < NZN), 1.0, 0.0).astype(BF16)
        inv_hi, inv_lo = hi_lo(STEP_SQUARED / ms[...])
        exf[x, 0:16] = dot(inv_hi, rep).astype(BF16)
        exf[x, 16:32] = dot(inv_lo, rep).astype(BF16)
        exf[x, 32:48] = prep[3, x]
        ids = ps[...]
        rows = pl.ds(pl.multiple_of(x * 16, 16), 16)
        for pair in range(13):
            port = halves(ids[:, 2 * pair:2 * pair + 1], ids[:, 2 * pair + 1:2 * pair + 2])
            oh[pair, rows, :] = jnp.where(port == lane % 64, 1.0, 0.0).astype(BF16)
        return carry

    lax.fori_loop(0, 5, prepare, 0)

    consts[0].wait()
    lhs = exf[...].reshape(240, 128)

    def widen(n, carry):
        cols = pl.ds(pl.multiple_of(n * 384, 384), 384)
        w = dot(lhs, ev[:, cols]).reshape(5, 48, 384)
        wf[:, 0:16, cols] = w[:, 0:16] + w[:, 16:32]
        wf[:, 16:32, cols] = w[:, 32:48]
        return carry

    lax.fori_loop(0, COLS // 384, widen, 0)

    def gather_points(layers):
        near = jnp.concatenate([txf[x, 0:8, COLS:] for x in layers], axis=0)
        far = jnp.concatenate([txf[x, 5:13, COLS:] for x in layers], axis=0)
        gathered = dot(jnp.concatenate([near, far], axis=1).astype(BF16), pv[...])
        for n, x in enumerate(layers):
            dsc[x] = gathered[8 * n:8 * n + 8]

    arrived(first[1])
    for x in range(5):
        txf[x, 10:11, :] = r1y[x:x + 1, :].astype(F32)
    consts[1].wait()
    gather_points(range(5))

    def fill(x, carry):
        def tile(m, ey, ez):
            kc = 15 * ez + m
            return txf[x, 5 * ey:5 * ey + 8, lane_tile(kc // 2)]

        for mp in range(9):
            for i, (e1, e2) in enumerate(PAIRS):
                both = []
                for m in (2 * mp, 2 * mp + 1):
                    a, b = tile(m, e1 // 5, e1 % 5), tile(m, e2 // 5, e2 % 5)
                    a_half, b_half = (15 * (e1 % 5) + m) % 2, (15 * (e2 % 5) + m) % 2
                    if a_half == 0 and b_half == 1:
                        both.append(halves(a, b))
                    elif a_half == 1 and b_half == 0:
                        both.append(pltpu.roll(halves(b, a), 64, 1))
                    elif a_half == 0:
                        both.append(halves(a, pltpu.roll(b, 64, 1)))
                    else:
                        both.append(halves(pltpu.roll(a, 64, 1), b))
                z[x, 16 * mp:16 * mp + 16, lane_tile(i)] = jnp.concatenate(both, axis=0).astype(BF16)
            both = [dsc[x, :, lane_tile(2 * mp)], dsc[x, :, lane_tile(2 * mp + 1)]]
            z[x, 16 * mp:16 * mp + 16, lane_tile(5)] = jnp.concatenate(both, axis=0).astype(BF16)
        return carry

    lax.fori_loop(0, 5, fill, 0)
    arrived(first[0])
    arrived(first[2])
    txf[5, 8:16, :] = jnp.zeros((8, WIDE), F32)
    for to, at in X_PACK:
        txf[(5,) + at] = r1x[to].astype(F32)
    for r in range(14):
        width = min(384, WIDE - r * 384)
        txf[5, 10:11, r * 384:r * 384 + width] = r1d[r:r + 1, 0:width].astype(F32)
    gather_points([5])
    fill(5, 0)
    consts[2].wait()

    def apply(x):
        rhs = z[...].reshape(864, 768)
        o[x] = sum(dot(kv[s, x], rhs) for s in range(SPLITS))

    def per_element(values):
        return [values[e // 5:e // 5 + 1, e % 5:e % 5 + 1] for e in range(10)]

    lams = per_element(lam_ref[0].astype(F32))
    mus = per_element(mu_ref[0].astype(F32))
    cells = per_element(cell_ref[0])
    lam_rows = [halves(lams[a], lams[b]) for a, b in PAIRS]
    mu_rows = [halves(mus[a], mus[b]) for a, b in PAIRS]
    lam_point = sum(jnp.where(lane == e, lams[e], 0.0) for e in range(10))
    mu_point = sum(jnp.where(lane == e, mus[e], 0.0) for e in range(10))
    sel_row = lax.broadcasted_iota(jnp.int32, (128, 128), 0)
    direction = jnp.concatenate([dir_ref[...], dir_ref[...]], axis=1)
    choose = jnp.concatenate(
        [
            jnp.where(
                (sel_row == halves(a, b)) & (direction == halves(cells[a], cells[b])), 1.0, 0.0
            ).astype(BF16)
            for a, b in PAIRS
        ],
        axis=1,
    )

    def assemble(x):
        tile5 = o[x, 144:288, lane_tile(5)]
        point = lam_point * o[x, 0:144, lane_tile(5)] + mu_point * tile5
        point = jnp.concatenate([point[8 * m:8 * m + 8] for m in range(18)], axis=1)
        point_hi = point.astype(BF16).astype(F32)
        fpb[x] = jnp.concatenate([point_hi, point - point_hi], axis=0).astype(BF16)
        k_hi, k_lo = hi_lo(tile5)
        source = dot(k_hi, choose) + dot(k_lo, choose)
        force = [
            lam_rows[i] * o[x, 0:144, lane_tile(i)]
            + mu_rows[i] * o[x, 144:288, lane_tile(i)]
            + source[:, lane_tile(i)]
            for i in range(5)
        ]
        fs[x, 8:16, :] = jnp.zeros((8, WIDE), F32)
        for ey in range(2):
            for t in range(39):
                stay, move = ([], []), ([], [])
                for h in range(2):
                    kc = 2 * t + h
                    ez, m = kc // 15, kc % 15
                    for ez_at, m_at in ((ez, m), (ez - 1, m + 15)):
                        if 0 <= ez_at < EZ and m_at < 18:
                            e = ey * 5 + ez_at
                            i = next(n for n, p in enumerate(PAIRS) if e in p)
                            half = PAIRS[i].index(e)
                            piece = force[i][8 * m_at:8 * m_at + 8]
                            (stay if half == h else move)[half].append(piece)
                zero = jnp.zeros((8, 128), F32)
                total = halves(sum(stay[0], zero), sum(stay[1], zero))
                if move[0] or move[1]:
                    total = total + pltpu.roll(
                        halves(sum(move[0], zero), sum(move[1], zero)), 64, 1
                    )
                if ey == 0:
                    fs[x, 0:8, lane_tile(t)] = total
                else:
                    fs[x, 5:13, lane_tile(t)] = fs[x, 5:13, lane_tile(t)] + total

    def place_point(x, values):
        values = values[0:8] + values[8:16]
        fs[x, 0:8, COLS:] = values[:, 0:128]
        fs[x, 5:13, COLS:] = fs[x, 5:13, COLS:] + values[:, 128:256]

    def pack_row(buffer, values):
        for r in range(-(-values.shape[1] // 384)):
            width = min(384, values.shape[1] - r * 384)
            buffer[r:r + 1, 0:width] = values[:, r * 384:r * 384 + width].astype(BF16)

    s2d[...] = jnp.zeros_like(s2d)
    s2y[...] = jnp.zeros_like(s2y)
    s2p[...] = jnp.zeros_like(s2p)
    apply(5)
    consts[3].wait()
    assemble(5)
    apply(0)
    place_point(5, dot(fpb[5], qv[...]))
    s2x[...] = fs[5].astype(BF16)
    pack_row(s2d, fs[5, 10:11, :])
    start(second[0])
    start(second[1])
    for x in range(5):
        if x < 4:
            apply(x + 1)
        assemble(x)
        pack_row(s2y.at[x], fs[x, 10:11, 0:COLS])
        start(second[3 + x])
    points = dot(fpb[0:5].reshape(80, 18 * 128), qv[...])
    for x in range(5):
        place_point(x, points[16 * x:16 * x + 16])
        s2p[x:x + 1, :] = fs[x, 10:11, COLS:].astype(BF16)
    start(second[2])

    def add_row(x, buffer, width):
        for r in range(-(-width // 384)):
            size = min(384, width - r * 384)
            cols = slice(r * 384, r * 384 + size)
            fs[x, 0:1, cols] = fs[x, 0:1, cols] + buffer[r:r + 1, 0:size].astype(F32)

    def finish(x, carry):
        rows = pl.ds(pl.multiple_of(x * 16, 16), 16)
        for pair in range(13):
            parts = []
            for t in range(3 * pair, 3 * pair + 3):
                cols = lane_tile(t)
                full = 2.0 * txf[x, :, cols] - tpf[x, :, cols] - wf[x, 0:16, cols] * fs[x, :, cols]
                tan_out[x, :, cols] = full[0:10].astype(BF16)
                parts.append(full * wf[x, 16:32, cols])
            a, b, c = parts
            amount = halves(a + pltpu.roll(a, 64, 1), c + pltpu.roll(c, 64, 1)) + b
            high, low = hi_lo(amount)
            uh[pair, rows, :] = high
            ul[pair, rows, :] = low
        return carry

    def finish_points(x, carry):
        fs[x, 0:1, COLS:] = fs[x, 0:1, COLS:] + r2p[x:x + 1, :].astype(F32)
        scale = exf[x, 0:16].astype(F32) + exf[x, 16:32].astype(F32)
        moved = (
            2.0 * txf[x, :, COLS:]
            - prep[1, x].astype(F32)
            + scale * (prep[2, x].astype(F32) - fs[x, :, COLS:])
        )
        disp_out[x] = moved.astype(BF16)
        return carry

    for x in (1, 2, 3):
        arrived(second[3 + x])
        add_row(x, r2y.at[x], COLS)
    lax.fori_loop(1, 4, finish, 0)
    arrived(second[0])
    arrived(second[1])
    arrived(second[3])
    fs[0] = fs[0] + r2x[...].astype(F32)
    add_row(0, r2y.at[0], COLS)
    add_row(0, r2d, WIDE)
    finish(0, 0)
    arrived(second[7])
    add_row(4, r2y.at[4], COLS)
    finish(4, 0)

    per_row = PORTS // ny
    slot = gx * nsrc_y + (gy - first_src)

    def port_copy(target_x, target_y, slot_at):
        return pltpu.make_async_remote_copy(
            src_ref=pbuf.at[target_y], dst_ref=prec.at[slot_at],
            send_sem=psend.at[target_x * ny + target_y], recv_sem=precv.at[slot_at],
            device_id=(target_x, target_y), device_id_type=MESH,
        )

    @pl.when(is_src)
    def _():
        onehot = oh[...].reshape(1040, 128)
        dims = (((0,), (0,)), ((), ()))
        square = lax.dot_general(
            onehot, uh[...].reshape(1040, 128), dims, preferred_element_type=F32
        ) + lax.dot_general(onehot, ul[...].reshape(1040, 128), dims, preferred_element_type=F32)
        amp = square[0:64] + pltpu.roll(square[64:128], 64, 1)
        for g in range(ny):
            pbuf[g] = jnp.zeros((8, 128), F32)
            pbuf[g, 0:per_row, :] = amp[g * per_row:(g + 1) * per_row]

        def send(t, carry):
            @pl.when(t != me)
            def _():
                port_copy(t // ny, t % ny, slot).start()
            return carry

        lax.fori_loop(0, n_all, send, 0)
        prec[slot] = pbuf[gy]

    arrived(second[2])
    for x in range(5):
        finish_points(x, 0)

    def collect(s, acc):
        @pl.when(jnp.logical_or(jnp.logical_not(is_src), s != slot))
        def _():
            port_copy(gx, gy, s).wait_recv()
        return acc + prec[s]

    acc = lax.fori_loop(0, nx * nsrc_y, collect, jnp.zeros((8, 128), F32))
    per_col = NT // nx
    mine = acc[0:per_row, 0:per_col]
    for h in range(1, nx):
        mine = jnp.where(gx == h, acc[0:per_row, h * per_col:(h + 1) * per_col], mine)
    port_out[...] = mine

    for item in first + second:
        sent(item)

    @pl.when(is_src)
    def _():
        def drain(t, carry):
            @pl.when(t != me)
            def _():
                port_copy(t // ny, t % ny, slot).wait_send()
            return carry

        lax.fori_loop(0, n_all, drain, 0)


def settle(tan, port, tan_out, port_out, sem):
    copies = [pltpu.make_async_copy(tan.at[x], tan_out.at[x], sem.at[x]) for x in range(5)]
    copies.append(pltpu.make_async_copy(port, port_out, sem.at[5]))
    for copy in copies:
        copy.start()
    for copy in copies:
        copy.wait()


def per_device(
    nx, ny,
    disp, disp_prev, tangent, tangent_prev, lame_lambda, lame_mu, node_mass, force,
    cell_block, direction_block, port_id, port_mode,
):
    rows = disp.shape[1]
    nsrc_y = -(-PORT_DEPTH // rows)
    stacked = jnp.stack([disp, disp_prev, force, port_mode]).transpose(0, 1, 2, 4, 3)
    stacked = jnp.pad(stacked, ((0, 0), (0, 0), (0, 16 - rows), (0, 1), (0, 32 - NZN)))
    prep = stacked.reshape(4, 5, 16, 128)
    expand, gather, scatter = layout_tables()
    tables = element_tables()
    nsrc = nx * nsrc_y
    vmem = pl.BlockSpec(memory_space=pltpu.VMEM)
    hbm = pl.BlockSpec(memory_space=pl.ANY)
    big = pltpu.VMEM((16, WIDE), BF16)
    small = pltpu.VMEM((16, 384), BF16)
    packed = pltpu.VMEM((16, 3200), BF16)
    rows5 = pltpu.VMEM((5, 16, 384), BF16)
    point = pltpu.VMEM((16, 128), BF16)
    tangent_next, moved, port_amp = pl.pallas_call(
        functools.partial(kernel, nx, ny, nsrc_y),
        out_shape=(
            jax.ShapeDtypeStruct(tangent.shape, BF16),
            jax.ShapeDtypeStruct((5, 16, 128), BF16),
            jax.ShapeDtypeStruct((PORTS // ny, NT // nx), F32),
        ),
        in_specs=[vmem] * 9 + [hbm] * 4,
        out_specs=(vmem, vmem, vmem),
        scratch_shapes=[
            pltpu.VMEM(tables.shape, BF16),
            pltpu.VMEM(expand.shape, BF16),
            pltpu.VMEM(gather.shape, BF16),
            pltpu.VMEM(scatter.shape, BF16),
            pltpu.SemaphoreType.DMA((4,)),
            pltpu.VMEM((6, 16, WIDE), F32),
            pltpu.VMEM((5, 16, COLS), F32),
            pltpu.VMEM((5, 48, 128), BF16),
            pltpu.VMEM((5, 32, COLS), F32),
            pltpu.VMEM((13, 80, 128), BF16),
            pltpu.VMEM((13, 80, 128), BF16),
            pltpu.VMEM((13, 80, 128), BF16),
            pltpu.VMEM((16, 128), F32),
            pltpu.VMEM((16, 128), jnp.int32),
            pltpu.VMEM((6, 8, 18 * 128), F32),
            pltpu.VMEM((6, 144, 768), BF16),
            pltpu.VMEM((6, 288, 768), F32),
            pltpu.VMEM((6, 16, WIDE), F32),
            pltpu.VMEM((6, 16, 18 * 128), BF16),
            packed, big, small, packed, big, small,
            big, rows5, small, point, big, rows5, small, point,
            pltpu.VMEM((ny, 8, 128), F32),
            pltpu.VMEM((nsrc, 8, 128), F32),
            pltpu.SemaphoreType.DMA((11,)),
            pltpu.SemaphoreType.DMA((11,)),
            pltpu.SemaphoreType.DMA((nx * ny,)),
            pltpu.SemaphoreType.DMA((nsrc,)),
        ],
        compiler_params=pltpu.CompilerParams(
            collective_id=0, has_side_effects=True, vmem_limit_bytes=56 * 1024 * 1024
        ),
    )(
        lame_lambda, lame_mu, cell_block, direction_block[None], tangent, tangent_prev, prep, node_mass, port_id,
        jnp.asarray(tables), jnp.asarray(expand), jnp.asarray(gather), jnp.asarray(scatter),
    )
    tangent_next, port_amp = pl.pallas_call(
        settle,
        out_shape=(
            jax.ShapeDtypeStruct(tangent_next.shape, BF16),
            jax.ShapeDtypeStruct(port_amp.shape, F32),
        ),
        in_specs=[hbm, hbm],
        out_specs=(hbm, hbm),
        scratch_shapes=[pltpu.SemaphoreType.DMA((6,))],
    )(tangent_next, port_amp)
    moved = moved.reshape(5, 16, 4, 32)[:, :rows, :3, :NZN].transpose(0, 1, 3, 2)
    return moved, tangent_next, port_amp


def solution(mesh):
    nx, ny = mesh.shape["gx"], mesh.shape["gy"]
    return jax.shard_map(
        functools.partial(per_device, nx, ny),
        mesh=mesh,
        in_specs=(
            P("gx", "gy", None, None),
            P("gx", "gy", None, None),
            P("gx", "gy", None),
            P("gx", "gy", None),
            P("gx", "gy", None),
            P("gx", "gy", None),
            P("gx", "gy", None),
            P("gx", "gy", None, None),
            P("gx", "gy", None),
            P(),
            P("gx", "gy", None),
            P("gx", "gy", None, None),
        ),
        out_specs=(P("gx", "gy", None, None), P("gx", "gy", None), P("gy", "gx")),
        check_vma=False,
    )
```

```python
import functools

import jax
import jax.numpy as jnp
import numpy as np
from jax import lax
from jax.experimental import pallas as pl
from jax.experimental.pallas import tpu as pltpu
from jax.sharding import PartitionSpec as P

PORTS = 64
PORT_DEPTH = 40
EZ = 5
NT = 64
NZN = 26
GLL_POINTS = np.array(
    [-1.0, -0.765055323929465, -0.285231516480645, 0.285231516480645, 0.765055323929465, 1.0]
)
GLL_WEIGHTS = np.array(
    [
        1.0 / 15.0,
        0.378474956297847,
        0.554858377035486,
        0.554858377035486,
        0.378474956297847,
        1.0 / 15.0,
    ]
)
STEP_SQUARED = 0.03
MESH = pl.DeviceIdType.MESH
F32 = jnp.float32
BF16 = jnp.bfloat16
COLS = 3 * NZN * NT
WIDE = COLS + 128
SPLITS = 2
PAIRS = ((0, 1), (2, 3), (5, 6), (7, 8), (4, 9))


def derivative_table():
    identity = np.eye(6)
    differences = GLL_POINTS[:, None] - GLL_POINTS[None, :] + identity
    barycentric = 1.0 / np.prod(differences, axis=1)
    matrix = barycentric[None, :] / barycentric[:, None] / differences
    matrix = matrix * (1.0 - identity)
    matrix = matrix - identity * matrix.sum(axis=1)[:, None]
    return matrix


def split_bf16(table):
    high = table.astype(jnp.bfloat16)
    low = (table - high.astype(np.float64)).astype(jnp.bfloat16)
    return [high, low]


def element_tables():
    d = derivative_table()
    eye = np.eye(6)
    ds = [
        np.kron(np.kron(d, eye), eye),
        np.kron(np.kron(eye, d), eye),
        np.kron(np.kron(eye, eye), d),
    ]
    w = np.kron(np.kron(GLL_WEIGHTS, GLL_WEIGHTS), GLL_WEIGHTS)[:, None]
    lap = sum(m.T @ (w * m) for m in ds)
    both = np.zeros((2, 216, 3, 216, 3))
    for c in range(3):
        for e in range(3):
            both[0, :, c, :, e] = ds[c].T @ (w * ds[e])
            both[1, :, c, :, e] = ds[e].T @ (w * ds[c]) + (lap if c == e else 0.0)
    both = both.reshape(2, 6, 6, 6, 3, 6, 6, 6, 3)
    both = both.transpose(0, 1, 3, 4, 2, 5, 7, 8, 6)
    both = both.reshape(2, 6, 108, 6, 108)
    both = np.pad(both, ((0, 0), (0, 0), (0, 4), (0, 0), (0, 4))).reshape(2, 6, 112, 672)
    both = both.transpose(1, 0, 2, 3).reshape(6, 224, 672)
    return np.stack(split_bf16(both)[:SPLITS])


def layout_tables():
    expand = np.zeros((128, NZN, 3, NT))
    for k in range(NZN):
        for c in range(3):
            expand[c * 32 + k, k, c, :] = 1.0
    gather = np.zeros((2, 128, 18, 128))
    for ey in range(2):
        for ez in range(EZ):
            for kz in range(6):
                for c in range(3):
                    gather[ey, c * 32 + 5 * ez + kz, kz * 3 + c, ey * 5 + ez] = 1.0
    gather = gather.reshape(256, 18 * 128)
    return (
        expand.reshape(128, COLS).astype(jnp.bfloat16),
        gather.astype(jnp.bfloat16),
        np.ascontiguousarray(gather.T).astype(jnp.bfloat16),
    )


X_PACK = (
    (np.s_[0:10, 0:3200], np.s_[0:10, 0:3200]),
    (np.s_[10:16, 0:1920], np.s_[0:6, 3200:5120]),
    (np.s_[10:14, 1920:3200], np.s_[6:10, 3200:4480]),
    (np.s_[14:16, 1920:2560], np.s_[6:8, 4480:5120]),
    (np.s_[14:16, 2560:3200], np.s_[8:10, 4480:5120]),
)


def lane_tile(t):
    return slice(t * 128, (t + 1) * 128)


def hi_lo(values):
    high = values.astype(BF16)
    return high, (values - high.astype(F32)).astype(BF16)


def dot(a, b):
    return jnp.dot(a, b, preferred_element_type=F32)


def kernel(
    nx, ny, nsrc_y,
    lam_ref, mu_ref, cell_ref, dir_ref, tan, tanp, prep, mass, pid, k_hbm, e_hbm, p_hbm, q_hbm,
    tan_out, disp_out, port_out,
    kv, ev, pv, qv, const_sem,
    txf, tpf, exf, wf, oh, oht, uu, ms, ps, dsc, z, o, zf, cf, fs, fpb,
    s1x, s1y, s1d, r1x, r1y, r1d, s2x, s2y, s2d, s2p, r2x, r2y, r2d, r2p,
    pbuf, prec, send_sem, recv_sem, psend, precv,
):
    gx = lax.axis_index("gx")
    gy = lax.axis_index("gy")
    consts = [
        pltpu.make_async_copy(a, b, const_sem.at[i])
        for i, (a, b) in enumerate(((e_hbm, ev), (p_hbm, pv), (k_hbm, kv), (q_hbm, qv)))
    ]
    for copy in consts:
        copy.start()

    x_lo, x_hi = gx > 0, gx < nx - 1
    y_lo, y_hi = gy > 0, gy < ny - 1
    first_src = ny - nsrc_y
    is_src = gy >= first_src
    n_all = nx * ny
    me = gx * ny + gy

    barrier = pltpu.get_barrier_semaphore()
    around = (
        (x_lo, -1, 0), (x_hi, 1, 0), (y_lo, 0, -1), (y_hi, 0, 1),
        (jnp.logical_and(x_lo, y_lo), -1, -1), (jnp.logical_and(x_hi, y_hi), 1, 1),
    )
    expected = jnp.int32(0)
    for there, dx, dy in around:
        @pl.when(there)
        def _(dx=dx, dy=dy):
            pl.semaphore_signal(barrier, inc=1, device_id=(gx + dx, gy + dy), device_id_type=MESH)
        expected = expected + there.astype(jnp.int32)

    def greet(s, carry):
        sx = s // nsrc_y
        sy = first_src + s % nsrc_y

        @pl.when(sx * ny + sy != me)
        def _():
            pl.semaphore_signal(barrier, inc=1, device_id=(sx, sy), device_id_type=MESH)
        return carry

    lax.fori_loop(0, nx * nsrc_y, greet, 0)
    expected = expected + is_src.astype(jnp.int32) * (n_all - 1)

    s1y[...] = jnp.zeros_like(s1y)
    s1d[...] = jnp.zeros_like(s1d)
    layer = jnp.concatenate([tan[0], prep[0, 0, 0:10, :]], axis=1)
    for to, at in X_PACK:
        s1x[to] = layer[at]
    for x in range(5):
        s1y[x:x + 1, 0:COLS] = tan[x, 0:1, :]
        s1y[x:x + 1, COLS:] = prep[0, x, 0:1, :]
    row = jnp.concatenate([tan[0, 0:1, :], prep[0, 0, 0:1, :]], axis=1)
    for r in range(14):
        width = min(384, WIDE - r * 384)
        s1d[r:r + 1, 0:width] = row[:, r * 384:r * 384 + width]

    pl.semaphore_wait(barrier, expected)

    def remote(index, src, dst, dx, dy):
        return pltpu.make_async_remote_copy(
            src_ref=src, dst_ref=dst, send_sem=send_sem.at[index], recv_sem=recv_sem.at[index],
            device_id=(gx + dx, gy + dy), device_id_type=MESH,
        )

    first = (
        (remote(0, s1x, r1x, -1, 0), x_lo, x_hi, r1x),
        (remote(1, s1y, r1y, 0, -1), y_lo, y_hi, r1y),
        (remote(2, s1d, r1d, -1, -1), jnp.logical_and(x_lo, y_lo), jnp.logical_and(x_hi, y_hi), r1d),
    )
    second = (
        (remote(3, s2x, r2x, 1, 0), x_hi, x_lo, r2x),
        (remote(4, s2d, r2d, 1, 1), jnp.logical_and(x_hi, y_hi), jnp.logical_and(x_lo, y_lo), r2d),
        (remote(5, s2p, r2p, 0, 1), y_hi, y_lo, r2p),
    ) + tuple(
        (remote(6 + x, s2y.at[x], r2y.at[x], 0, 1), y_hi, y_lo, r2y.at[x]) for x in range(5)
    )

    def start(item):
        copy, sends, _, _ = item

        @pl.when(sends)
        def _():
            copy.start()

    def arrived(item):
        copy, _, receives, buffer = item

        @pl.when(receives)
        def _():
            copy.wait_recv()

        @pl.when(jnp.logical_not(receives))
        def _():
            buffer[...] = jnp.zeros_like(buffer)

    def sent(item):
        copy, sends, _, _ = item

        @pl.when(sends)
        def _():
            copy.wait_send()

    for item in first:
        start(item)

    lane = lax.broadcasted_iota(jnp.int32, (1, 128), 1)
    low_half = lane < 64

    def halves(a, b):
        return jnp.where(low_half, a, b)

    def prepare(x, carry):
        txf[x, 8:16, :] = jnp.zeros((8, WIDE), F32)
        tpf[x, 8:16, :] = jnp.zeros((8, COLS), F32)
        txf[x, 0:10, 0:COLS] = tan[x].astype(F32)
        txf[x, :, COLS:] = prep[0, x].astype(F32)
        tpf[x, 0:10, :] = tanp[x].astype(F32)
        ms[...] = jnp.ones_like(ms)
        ps[...] = jnp.full(ps.shape, PORTS, jnp.int32)
        ms[0:10, 0:NZN] = mass[x]
        ps[0:10, 0:NZN] = pid[x]
        rep_row = lax.broadcasted_iota(jnp.int32, (128, 128), 0)
        rep_col = lax.broadcasted_iota(jnp.int32, (128, 128), 1)
        rep = jnp.where((rep_col % 32 == rep_row) & (rep_row < NZN), 1.0, 0.0).astype(BF16)
        inv_hi, inv_lo = hi_lo(STEP_SQUARED / ms[...])
        exf[x, 0:16] = dot(inv_hi, rep).astype(BF16)
        exf[x, 16:32] = dot(inv_lo, rep).astype(BF16)
        exf[x, 32:48] = prep[3, x]
        ids = ps[...]
        rows = pl.ds(pl.multiple_of(x * 16, 16), 16)
        for pair in range(13):
            port = halves(ids[:, 2 * pair:2 * pair + 1], ids[:, 2 * pair + 1:2 * pair + 2])
            oh[pair, rows, :] = jnp.where(port == lane % 64, 1.0, 0.0)
        return carry

    lax.fori_loop(0, 5, prepare, 0)

    @pl.when(is_src)
    def _():
        oht[...] = oh[...].reshape(1040, 128).T.astype(BF16)

    consts[0].wait()
    lhs = exf[...].reshape(240, 128)

    def widen(n, carry):
        cols = pl.ds(pl.multiple_of(n * 384, 384), 384)
        w = dot(lhs, ev[:, cols]).reshape(5, 48, 384)
        wf[:, 0:16, cols] = w[:, 0:16] + w[:, 16:32]
        wf[:, 16:32, cols] = w[:, 32:48]
        return carry

    lax.fori_loop(0, COLS // 384, widen, 0)

    def gather_points(layers):
        near = jnp.concatenate([txf[x, 0:8, COLS:] for x in layers], axis=0)
        far = jnp.concatenate([txf[x, 5:13, COLS:] for x in layers], axis=0)
        gathered = dot(jnp.concatenate([near, far], axis=1).astype(BF16), pv[...])
        for n, x in enumerate(layers):
            dsc[x] = gathered[8 * n:8 * n + 8]

    arrived(first[1])
    for x in range(5):
        txf[x, 10:11, :] = r1y[x:x + 1, :].astype(F32)
    consts[1].wait()
    gather_points(range(5))

    zf[96:112, :] = jnp.zeros((16, 768), F32)

    def fill(x, carry):
        def tile(m, ey, ez):
            kc = 15 * ez + m
            return txf[x, 5 * ey:5 * ey + 8, lane_tile(kc // 2)]

        for m in range(18):
            rows = slice(6 * m, 6 * m + 8)
            for i, (e1, e2) in enumerate(PAIRS):
                a, b = tile(m, e1 // 5, e1 % 5), tile(m, e2 // 5, e2 % 5)
                a_half, b_half = (15 * (e1 % 5) + m) % 2, (15 * (e2 % 5) + m) % 2
                if a_half == 0 and b_half == 1:
                    both = halves(a, b)
                elif a_half == 1 and b_half == 0:
                    both = pltpu.roll(halves(b, a), 64, 1)
                elif a_half == 0:
                    both = halves(a, pltpu.roll(b, 64, 1))
                else:
                    both = halves(pltpu.roll(a, 64, 1), b)
                zf[rows, lane_tile(i)] = both
            zf[rows, lane_tile(5)] = dsc[x, :, lane_tile(m)]
        z[x] = zf[...].astype(BF16)
        return carry

    lax.fori_loop(0, 5, fill, 0)
    arrived(first[0])
    arrived(first[2])
    txf[5, 8:16, :] = jnp.zeros((8, WIDE), F32)
    for to, at in X_PACK:
        txf[(5,) + at] = r1x[to].astype(F32)
    for r in range(14):
        width = min(384, WIDE - r * 384)
        txf[5, 10:11, r * 384:r * 384 + width] = r1d[r:r + 1, 0:width].astype(F32)
    gather_points([5])
    fill(5, 0)
    consts[2].wait()

    def apply(x):
        rhs = z[...].reshape(672, 768)
        o[x] = sum(dot(kv[s, x], rhs) for s in range(SPLITS))

    def per_element(values):
        return [values[e // 5:e // 5 + 1, e % 5:e % 5 + 1] for e in range(10)]

    lams = per_element(lam_ref[0].astype(F32))
    mus = per_element(mu_ref[0].astype(F32))
    cells = per_element(cell_ref[0])
    lam_rows = [halves(lams[a], lams[b]) for a, b in PAIRS]
    mu_rows = [halves(mus[a], mus[b]) for a, b in PAIRS]
    lam_point = sum(jnp.where(lane == e, lams[e], 0.0) for e in range(10))
    mu_point = sum(jnp.where(lane == e, mus[e], 0.0) for e in range(10))
    sel_row = lax.broadcasted_iota(jnp.int32, (128, 128), 0)
    direction = jnp.concatenate([dir_ref[...], dir_ref[...]], axis=1)
    choose = jnp.concatenate(
        [
            jnp.where(
                (sel_row == halves(a, b)) & (direction == halves(cells[a], cells[b])), 1.0, 0.0
            ).astype(BF16)
            for a, b in PAIRS
        ],
        axis=1,
    )

    first_row = lax.broadcasted_iota(jnp.int32, (8, 128), 0) == 0

    def merged(pieces):
        low, high = [functools.reduce(jnp.add, p) if p else 0.0 for p in pieces]
        return halves(low, high)

    def assemble(x):
        tile5 = o[x, 112:224, lane_tile(5)]
        cf[0:112, lane_tile(5)] = lam_point * o[x, 0:112, lane_tile(5)] + mu_point * tile5
        point = jnp.concatenate([cf[6 * m:6 * m + 8, lane_tile(5)] for m in range(18)], axis=1)
        point_hi = point.astype(BF16).astype(F32)
        fpb[x] = jnp.concatenate([point_hi, point - point_hi], axis=0).astype(BF16)
        k_hi, k_lo = hi_lo(tile5)
        source = dot(k_hi, choose) + dot(k_lo, choose)
        for i in range(5):
            cf[0:112, lane_tile(i)] = (
                lam_rows[i] * o[x, 0:112, lane_tile(i)]
                + mu_rows[i] * o[x, 112:224, lane_tile(i)]
                + source[:, lane_tile(i)]
            )
        fs[x, 8:16, :] = jnp.zeros((8, WIDE), F32)
        for ey in range(2):
            for t in range(39):
                stay, move = ([], []), ([], [])
                for h in range(2):
                    kc = 2 * t + h
                    ez, m = kc // 15, kc % 15
                    for ez_at, m_at in ((ez, m), (ez - 1, m + 15)):
                        if 0 <= ez_at < EZ and m_at < 18:
                            e = ey * 5 + ez_at
                            i = next(n for n, p in enumerate(PAIRS) if e in p)
                            half = PAIRS[i].index(e)
                            piece = cf[6 * m_at:6 * m_at + 8, lane_tile(i)]
                            (stay if half == h else move)[half].append(piece)
                total = merged(stay)
                if move[0] or move[1]:
                    total = total + pltpu.roll(merged(move), 64, 1)
                if ey == 0:
                    fs[x, 0:8, lane_tile(t)] = total
                else:
                    shared = jnp.where(first_row, fs[x, 5:13, lane_tile(t)], 0.0)
                    fs[x, 5:13, lane_tile(t)] = shared + total

    def place_point(x, values):
        values = values[0:8] + values[8:16]
        fs[x, 0:8, COLS:] = values[:, 0:128]
        shared = jnp.where(first_row, fs[x, 5:13, COLS:], 0.0)
        fs[x, 5:13, COLS:] = shared + values[:, 128:256]

    def pack_row(buffer, values):
        for r in range(-(-values.shape[1] // 384)):
            width = min(384, values.shape[1] - r * 384)
            buffer[r:r + 1, 0:width] = values[:, r * 384:r * 384 + width].astype(BF16)

    s2d[...] = jnp.zeros_like(s2d)
    s2y[...] = jnp.zeros_like(s2y)
    s2p[...] = jnp.zeros_like(s2p)
    apply(5)
    consts[3].wait()
    assemble(5)
    apply(0)
    place_point(5, dot(fpb[5], qv[...]))
    s2x[...] = fs[5].astype(BF16)
    pack_row(s2d, fs[5, 10:11, :])
    start(second[0])
    start(second[1])
    for x in range(5):
        if x < 4:
            apply(x + 1)
        assemble(x)
        pack_row(s2y.at[x], fs[x, 10:11, 0:COLS])
        start(second[3 + x])
    points = dot(fpb[0:5].reshape(80, 18 * 128), qv[...])
    for x in range(5):
        place_point(x, points[16 * x:16 * x + 16])
        s2p[x:x + 1, :] = fs[x, 10:11, COLS:].astype(BF16)
    start(second[2])

    def add_row(x, buffer, width):
        for r in range(-(-width // 384)):
            size = min(384, width - r * 384)
            cols = slice(r * 384, r * 384 + size)
            fs[x, 0:1, cols] = fs[x, 0:1, cols] + buffer[r:r + 1, 0:size].astype(F32)

    def finish(x, carry):
        rows = pl.ds(pl.multiple_of(x * 16, 16), 16)
        for pair in range(13):
            parts = []
            for t in range(3 * pair, 3 * pair + 3):
                cols = lane_tile(t)
                full = 2.0 * txf[x, :, cols] - tpf[x, :, cols] - wf[x, 0:16, cols] * fs[x, :, cols]
                tan_out[x, :, cols] = full[0:10].astype(BF16)
                parts.append(full * wf[x, 16:32, cols])
            a, b, c = parts
            amount = halves(a + pltpu.roll(a, 64, 1), c + pltpu.roll(c, 64, 1)) + b
            high, low = hi_lo(amount)
            uu[pair, rows, 0:128] = high
            uu[pair, rows, 128:256] = low
        return carry

    def finish_points(x, carry):
        fs[x, 0:1, COLS:] = fs[x, 0:1, COLS:] + r2p[x:x + 1, :].astype(F32)
        scale = exf[x, 0:16].astype(F32) + exf[x, 16:32].astype(F32)
        moved = (
            2.0 * txf[x, :, COLS:]
            - prep[1, x].astype(F32)
            + scale * (prep[2, x].astype(F32) - fs[x, :, COLS:])
        )
        disp_out[x] = moved.astype(BF16)
        return carry

    for x in (1, 2, 3):
        arrived(second[3 + x])
        add_row(x, r2y.at[x], COLS)
    lax.fori_loop(1, 4, finish, 0)
    arrived(second[0])
    arrived(second[1])
    arrived(second[3])
    fs[0] = fs[0] + r2x[...].astype(F32)
    add_row(0, r2y.at[0], COLS)
    add_row(0, r2d, WIDE)
    finish(0, 0)
    arrived(second[7])
    add_row(4, r2y.at[4], COLS)
    finish(4, 0)

    per_row = PORTS // ny
    slot = gx * nsrc_y + (gy - first_src)

    def port_copy(target_x, target_y, slot_at):
        return pltpu.make_async_remote_copy(
            src_ref=pbuf.at[target_y], dst_ref=prec.at[slot_at],
            send_sem=psend.at[target_x * ny + target_y], recv_sem=precv.at[slot_at],
            device_id=(target_x, target_y), device_id_type=MESH,
        )

    @pl.when(is_src)
    def _():
        square = dot(oht[...], uu[...].reshape(1040, 256))
        square = square[:, 0:128] + square[:, 128:256]
        amp = square[0:64] + pltpu.roll(square[64:128], 64, 1)
        for g in range(ny):
            pbuf[g] = jnp.zeros((8, 128), F32)
            pbuf[g, 0:per_row, :] = amp[g * per_row:(g + 1) * per_row]

        def send(t, carry):
            @pl.when(t != me)
            def _():
                port_copy(t // ny, t % ny, slot).start()
            return carry

        lax.fori_loop(0, n_all, send, 0)
        prec[slot] = pbuf[gy]

    arrived(second[2])
    for x in range(5):
        finish_points(x, 0)

    def collect(s, acc):
        @pl.when(jnp.logical_or(jnp.logical_not(is_src), s != slot))
        def _():
            port_copy(gx, gy, s).wait_recv()
        return acc + prec[s]

    acc = lax.fori_loop(0, nx * nsrc_y, collect, jnp.zeros((8, 128), F32))
    per_col = NT // nx
    mine = acc[0:per_row, 0:per_col]
    for h in range(1, nx):
        mine = jnp.where(gx == h, acc[0:per_row, h * per_col:(h + 1) * per_col], mine)
    port_out[...] = mine

    for item in first + second:
        sent(item)

    @pl.when(is_src)
    def _():
        def drain(t, carry):
            @pl.when(t != me)
            def _():
                port_copy(t // ny, t % ny, slot).wait_send()
            return carry

        lax.fori_loop(0, n_all, drain, 0)


def settle(tan, port, tan_out, port_out):
    tan_out[...] = tan[...]
    port_out[...] = port[...]


def per_device(
    nx, ny,
    disp, disp_prev, tangent, tangent_prev, lame_lambda, lame_mu, node_mass, force,
    cell_block, direction_block, port_id, port_mode,
):
    rows = disp.shape[1]
    nsrc_y = -(-PORT_DEPTH // rows)
    stacked = jnp.stack([disp, disp_prev, force, port_mode]).transpose(0, 1, 2, 4, 3)
    stacked = jnp.pad(stacked, ((0, 0), (0, 0), (0, 16 - rows), (0, 1), (0, 32 - NZN)))
    prep = stacked.reshape(4, 5, 16, 128)
    expand, gather, scatter = layout_tables()
    tables = element_tables()
    nsrc = nx * nsrc_y
    vmem = pl.BlockSpec(memory_space=pltpu.VMEM)
    hbm = pl.BlockSpec(memory_space=pl.ANY)
    big = pltpu.VMEM((16, WIDE), BF16)
    small = pltpu.VMEM((16, 384), BF16)
    packed = pltpu.VMEM((16, 3200), BF16)
    rows5 = pltpu.VMEM((5, 16, 384), BF16)
    point = pltpu.VMEM((16, 128), BF16)
    tangent_next, moved, port_amp = pl.pallas_call(
        functools.partial(kernel, nx, ny, nsrc_y),
        out_shape=(
            jax.ShapeDtypeStruct(tangent.shape, BF16),
            jax.ShapeDtypeStruct((5, 16, 128), BF16),
            jax.ShapeDtypeStruct((PORTS // ny, NT // nx), F32),
        ),
        in_specs=[vmem] * 9 + [hbm] * 4,
        out_specs=(vmem, vmem, vmem),
        scratch_shapes=[
            pltpu.VMEM(tables.shape, BF16),
            pltpu.VMEM(expand.shape, BF16),
            pltpu.VMEM(gather.shape, BF16),
            pltpu.VMEM(scatter.shape, BF16),
            pltpu.SemaphoreType.DMA((4,)),
            pltpu.VMEM((6, 16, WIDE), F32),
            pltpu.VMEM((5, 16, COLS), F32),
            pltpu.VMEM((5, 48, 128), BF16),
            pltpu.VMEM((5, 32, COLS), F32),
            pltpu.VMEM((13, 80, 128), F32),
            pltpu.VMEM((128, 1040), BF16),
            pltpu.VMEM((13, 80, 256), BF16),
            pltpu.VMEM((16, 128), F32),
            pltpu.VMEM((16, 128), jnp.int32),
            pltpu.VMEM((6, 8, 18 * 128), F32),
            pltpu.VMEM((6, 112, 768), BF16),
            pltpu.VMEM((6, 224, 768), F32),
            pltpu.VMEM((112, 768), F32),
            pltpu.VMEM((112, 768), F32),
            pltpu.VMEM((6, 16, WIDE), F32),
            pltpu.VMEM((6, 16, 18 * 128), BF16),
            packed, big, small, packed, big, small,
            big, rows5, small, point, big, rows5, small, point,
            pltpu.VMEM((ny, 8, 128), F32),
            pltpu.VMEM((nsrc, 8, 128), F32),
            pltpu.SemaphoreType.DMA((11,)),
            pltpu.SemaphoreType.DMA((11,)),
            pltpu.SemaphoreType.DMA((nx * ny,)),
            pltpu.SemaphoreType.DMA((nsrc,)),
        ],
        compiler_params=pltpu.CompilerParams(
            collective_id=0, has_side_effects=True, vmem_limit_bytes=56 * 1024 * 1024
        ),
    )(
        lame_lambda, lame_mu, cell_block, direction_block[None], tangent, tangent_prev, prep, node_mass, port_id,
        jnp.asarray(tables), jnp.asarray(expand), jnp.asarray(gather), jnp.asarray(scatter),
    )
    tangent_next, port_amp = pl.pallas_call(
        settle,
        out_shape=(
            jax.ShapeDtypeStruct(tangent_next.shape, BF16),
            jax.ShapeDtypeStruct(port_amp.shape, F32),
        ),
        in_specs=[vmem, vmem],
        out_specs=(vmem, vmem),
    )(tangent_next, port_amp)
    moved = moved.reshape(5, 16, 4, 32)[:, :rows, :3, :NZN].transpose(0, 1, 3, 2)
    return moved, tangent_next, port_amp


def solution(mesh):
    nx, ny = mesh.shape["gx"], mesh.shape["gy"]
    return jax.shard_map(
        functools.partial(per_device, nx, ny),
        mesh=mesh,
        in_specs=(
            P("gx", "gy", None, None),
            P("gx", "gy", None, None),
            P("gx", "gy", None),
            P("gx", "gy", None),
            P("gx", "gy", None),
            P("gx", "gy", None),
            P("gx", "gy", None),
            P("gx", "gy", None, None),
            P("gx", "gy", None),
            P(),
            P("gx", "gy", None),
            P("gx", "gy", None, None),
        ),
        out_specs=(P("gx", "gy", None, None), P("gx", "gy", None), P("gy", "gx")),
        check_vma=False,
    )
```

```python
import functools

import jax
import jax.numpy as jnp
import numpy as np
from jax import lax
from jax.experimental import pallas as pl
from jax.experimental.pallas import tpu as pltpu
from jax.sharding import PartitionSpec as P

PORTS = 64
PORT_DEPTH = 40
EZ = 5
NT = 64
NZN = 26
GLL_POINTS = np.array(
    [-1.0, -0.765055323929465, -0.285231516480645, 0.285231516480645, 0.765055323929465, 1.0]
)
GLL_WEIGHTS = np.array(
    [
        1.0 / 15.0,
        0.378474956297847,
        0.554858377035486,
        0.554858377035486,
        0.378474956297847,
        1.0 / 15.0,
    ]
)
STEP_SQUARED = 0.03
MESH = pl.DeviceIdType.MESH
F32 = jnp.float32
BF16 = jnp.bfloat16
COLS = 3 * NZN * NT
WIDE = COLS + 128
SPLITS = 2
PAIRS = ((0, 1), (2, 3), (5, 6), (7, 8), (4, 9))


def derivative_table():
    identity = np.eye(6)
    differences = GLL_POINTS[:, None] - GLL_POINTS[None, :] + identity
    barycentric = 1.0 / np.prod(differences, axis=1)
    matrix = barycentric[None, :] / barycentric[:, None] / differences
    matrix = matrix * (1.0 - identity)
    matrix = matrix - identity * matrix.sum(axis=1)[:, None]
    return matrix


def split_bf16(table):
    high = table.astype(jnp.bfloat16)
    low = (table - high.astype(np.float64)).astype(jnp.bfloat16)
    return [high, low]


def element_tables():
    d = derivative_table()
    eye = np.eye(6)
    ds = [
        np.kron(np.kron(d, eye), eye),
        np.kron(np.kron(eye, d), eye),
        np.kron(np.kron(eye, eye), d),
    ]
    w = np.kron(np.kron(GLL_WEIGHTS, GLL_WEIGHTS), GLL_WEIGHTS)[:, None]
    lap = sum(m.T @ (w * m) for m in ds)
    both = np.zeros((2, 216, 3, 216, 3))
    for c in range(3):
        for e in range(3):
            both[0, :, c, :, e] = ds[c].T @ (w * ds[e])
            both[1, :, c, :, e] = ds[e].T @ (w * ds[c]) + (lap if c == e else 0.0)
    both = both.reshape(2, 6, 6, 6, 3, 6, 6, 6, 3)
    both = both.transpose(0, 1, 3, 4, 2, 5, 7, 8, 6)
    both = both.reshape(2, 6, 108, 6, 108)
    both = np.pad(both, ((0, 0), (0, 0), (0, 4), (0, 0), (0, 4))).reshape(2, 6, 112, 672)
    both = both.transpose(1, 0, 2, 3).reshape(6, 224, 672)
    return np.stack(split_bf16(both)[:SPLITS])


def layout_tables():
    expand = np.zeros((128, NZN, 3, NT))
    for k in range(NZN):
        for c in range(3):
            expand[c * 32 + k, k, c, :] = 1.0
    gather = np.zeros((2, 128, 18, 128))
    for ey in range(2):
        for ez in range(EZ):
            for kz in range(6):
                for c in range(3):
                    gather[ey, c * 32 + 5 * ez + kz, kz * 3 + c, ey * 5 + ez] = 1.0
    gather = gather.reshape(256, 18 * 128)
    return (
        expand.reshape(128, COLS).astype(jnp.bfloat16),
        gather.astype(jnp.bfloat16),
        np.ascontiguousarray(gather.T).astype(jnp.bfloat16),
    )


X_PACK = (
    (np.s_[0:10, 0:3200], np.s_[0:10, 0:3200]),
    (np.s_[10:16, 0:1920], np.s_[0:6, 3200:5120]),
    (np.s_[10:14, 1920:3200], np.s_[6:10, 3200:4480]),
    (np.s_[14:16, 1920:2560], np.s_[6:8, 4480:5120]),
    (np.s_[14:16, 2560:3200], np.s_[8:10, 4480:5120]),
)


def lane_tile(t):
    return slice(t * 128, (t + 1) * 128)


def hi_lo(values):
    high = values.astype(BF16)
    return high, (values - high.astype(F32)).astype(BF16)


def dot(a, b):
    return jnp.dot(a, b, preferred_element_type=F32)


def kernel(
    nx, ny, nsrc_y,
    lam_ref, mu_ref, cell_ref, dir_ref, tan_hbm, tanp_hbm, now, past, load, mode, mass, pid, k_hbm, e_hbm, p_hbm, q_hbm,
    tan_hbm_out, disp_out, port_out,
    tan, tanp, tan_out, out_sem, prep,
    kv, ev, pv, qv, const_sem,
    txf, tpf, exf, wf, oh, oht, uu, ms, ps, dsc, z, o, zf, cf, fs, fpb,
    s1x, s1y, s1d, r1x, r1y, r1d, s2x, s2y, s2d, s2p, r2x, r2y, r2d, r2p,
    pbuf, prec, send_sem, recv_sem, psend, precv,
):
    gx = lax.axis_index("gx")
    gy = lax.axis_index("gy")
    consts = [
        pltpu.make_async_copy(a, b, const_sem.at[i])
        for i, (a, b) in enumerate(
            (
                (e_hbm, ev), (p_hbm, pv), (k_hbm, kv), (q_hbm, qv),
                (tan_hbm, tan), (tanp_hbm, tanp),
            )
        )
    ]
    for i in (4, 5, 0, 1, 2, 3):
        consts[i].start()

    x_lo, x_hi = gx > 0, gx < nx - 1
    y_lo, y_hi = gy > 0, gy < ny - 1
    first_src = ny - nsrc_y
    is_src = gy >= first_src
    n_all = nx * ny
    me = gx * ny + gy

    barrier = pltpu.get_barrier_semaphore()
    around = (
        (x_lo, -1, 0), (x_hi, 1, 0), (y_lo, 0, -1), (y_hi, 0, 1),
        (jnp.logical_and(x_lo, y_lo), -1, -1), (jnp.logical_and(x_hi, y_hi), 1, 1),
    )
    expected = jnp.int32(0)
    for there, dx, dy in around:
        @pl.when(there)
        def _(dx=dx, dy=dy):
            pl.semaphore_signal(barrier, inc=1, device_id=(gx + dx, gy + dy), device_id_type=MESH)
        expected = expected + there.astype(jnp.int32)

    def greet(s, carry):
        sx = s // nsrc_y
        sy = first_src + s % nsrc_y

        @pl.when(sx * ny + sy != me)
        def _():
            pl.semaphore_signal(barrier, inc=1, device_id=(sx, sy), device_id_type=MESH)
        return carry

    lax.fori_loop(0, nx * nsrc_y, greet, 0)
    expected = expected + is_src.astype(jnp.int32) * (n_all - 1)

    def lanes(source, index, x):
        for c in range(3):
            prep[index, x, 0:10, 32 * c:32 * c + NZN] = source[x, :, c, :].astype(F32)

    prep[...] = jnp.zeros_like(prep)
    for x in range(5):
        lanes(now, 0, x)

    consts[4].wait()
    s1y[...] = jnp.zeros_like(s1y)
    s1d[...] = jnp.zeros_like(s1d)
    layer = jnp.concatenate([tan[0], prep[0, 0, 0:10, :].astype(BF16)], axis=1)
    for to, at in X_PACK:
        s1x[to] = layer[at]
    for x in range(5):
        s1y[x:x + 1, 0:COLS] = tan[x, 0:1, :]
        s1y[x:x + 1, COLS:] = prep[0, x, 0:1, :].astype(BF16)
    row = jnp.concatenate([tan[0, 0:1, :], prep[0, 0, 0:1, :].astype(BF16)], axis=1)
    for r in range(14):
        width = min(384, WIDE - r * 384)
        s1d[r:r + 1, 0:width] = row[:, r * 384:r * 384 + width]

    pl.semaphore_wait(barrier, expected)

    def remote(index, src, dst, dx, dy):
        return pltpu.make_async_remote_copy(
            src_ref=src, dst_ref=dst, send_sem=send_sem.at[index], recv_sem=recv_sem.at[index],
            device_id=(gx + dx, gy + dy), device_id_type=MESH,
        )

    first = (
        (remote(0, s1x, r1x, -1, 0), x_lo, x_hi, r1x),
        (remote(1, s1y, r1y, 0, -1), y_lo, y_hi, r1y),
        (remote(2, s1d, r1d, -1, -1), jnp.logical_and(x_lo, y_lo), jnp.logical_and(x_hi, y_hi), r1d),
    )
    second = (
        (remote(3, s2x, r2x, 1, 0), x_hi, x_lo, r2x),
        (remote(4, s2d, r2d, 1, 1), jnp.logical_and(x_hi, y_hi), jnp.logical_and(x_lo, y_lo), r2d),
        (remote(5, s2p, r2p, 0, 1), y_hi, y_lo, r2p),
    ) + tuple(
        (remote(6 + x, s2y.at[x], r2y.at[x], 0, 1), y_hi, y_lo, r2y.at[x]) for x in range(5)
    )

    def start(item):
        copy, sends, _, _ = item

        @pl.when(sends)
        def _():
            copy.start()

    def arrived(item):
        copy, _, receives, buffer = item

        @pl.when(receives)
        def _():
            copy.wait_recv()

        @pl.when(jnp.logical_not(receives))
        def _():
            buffer[...] = jnp.zeros_like(buffer)

    def sent(item):
        copy, sends, _, _ = item

        @pl.when(sends)
        def _():
            copy.wait_send()

    for item in first:
        start(item)

    lane = lax.broadcasted_iota(jnp.int32, (1, 128), 1)
    low_half = lane < 64

    def halves(a, b):
        return jnp.where(low_half, a, b)

    def prepare(x, carry):
        txf[x, 8:16, :] = jnp.zeros((8, WIDE), F32)
        tpf[x, 8:16, :] = jnp.zeros((8, COLS), F32)
        txf[x, 0:10, 0:COLS] = tan[x].astype(F32)
        txf[x, :, COLS:] = prep[0, x]
        for index, source in ((1, past), (2, load), (3, mode)):
            lanes(source, index, x)
        tpf[x, 0:10, :] = tanp[x].astype(F32)
        ms[...] = jnp.ones_like(ms)
        ps[...] = jnp.full(ps.shape, PORTS, jnp.int32)
        ms[0:10, 0:NZN] = mass[x]
        ps[0:10, 0:NZN] = pid[x]
        rep_row = lax.broadcasted_iota(jnp.int32, (128, 128), 0)
        rep_col = lax.broadcasted_iota(jnp.int32, (128, 128), 1)
        rep = jnp.where((rep_col % 32 == rep_row) & (rep_row < NZN), 1.0, 0.0).astype(BF16)
        inv_hi, inv_lo = hi_lo(STEP_SQUARED / ms[...])
        exf[x, 0:16] = dot(inv_hi, rep).astype(BF16)
        exf[x, 16:32] = dot(inv_lo, rep).astype(BF16)
        exf[x, 32:48] = prep[3, x].astype(BF16)
        ids = ps[...]
        rows = pl.ds(pl.multiple_of(x * 16, 16), 16)
        for pair in range(13):
            port = halves(ids[:, 2 * pair:2 * pair + 1], ids[:, 2 * pair + 1:2 * pair + 2])
            oh[pair, rows, :] = jnp.where(port == lane % 64, 1.0, 0.0)
        return carry

    consts[5].wait()
    lax.fori_loop(0, 5, prepare, 0)

    @pl.when(is_src)
    def _():
        oht[...] = oh[...].reshape(1040, 128).T.astype(BF16)

    consts[0].wait()
    lhs = exf[...].reshape(240, 128)

    def widen(n, carry):
        cols = pl.ds(pl.multiple_of(n * 384, 384), 384)
        w = dot(lhs, ev[:, cols]).reshape(5, 48, 384)
        wf[:, 0:16, cols] = w[:, 0:16] + w[:, 16:32]
        wf[:, 16:32, cols] = w[:, 32:48]
        return carry

    lax.fori_loop(0, COLS // 384, widen, 0)

    def gather_points(layers):
        near = jnp.concatenate([txf[x, 0:8, COLS:] for x in layers], axis=0)
        far = jnp.concatenate([txf[x, 5:13, COLS:] for x in layers], axis=0)
        gathered = dot(jnp.concatenate([near, far], axis=1).astype(BF16), pv[...])
        for n, x in enumerate(layers):
            dsc[x] = gathered[8 * n:8 * n + 8]

    arrived(first[1])
    for x in range(5):
        txf[x, 10:11, :] = r1y[x:x + 1, :].astype(F32)
    consts[1].wait()
    gather_points(range(5))

    zf[96:112, :] = jnp.zeros((16, 768), F32)

    def fill(x, carry):
        def tile(m, ey, ez):
            kc = 15 * ez + m
            return txf[x, 5 * ey:5 * ey + 8, lane_tile(kc // 2)]

        for m in range(18):
            rows = slice(6 * m, 6 * m + 8)
            for i, (e1, e2) in enumerate(PAIRS):
                a, b = tile(m, e1 // 5, e1 % 5), tile(m, e2 // 5, e2 % 5)
                a_half, b_half = (15 * (e1 % 5) + m) % 2, (15 * (e2 % 5) + m) % 2
                if a_half == 0 and b_half == 1:
                    both = halves(a, b)
                elif a_half == 1 and b_half == 0:
                    both = pltpu.roll(halves(b, a), 64, 1)
                elif a_half == 0:
                    both = halves(a, pltpu.roll(b, 64, 1))
                else:
                    both = halves(pltpu.roll(a, 64, 1), b)
                zf[rows, lane_tile(i)] = both
            zf[rows, lane_tile(5)] = dsc[x, :, lane_tile(m)]
        z[x] = zf[...].astype(BF16)
        return carry

    lax.fori_loop(0, 5, fill, 0)
    arrived(first[0])
    arrived(first[2])
    txf[5, 8:16, :] = jnp.zeros((8, WIDE), F32)
    for to, at in X_PACK:
        txf[(5,) + at] = r1x[to].astype(F32)
    for r in range(14):
        width = min(384, WIDE - r * 384)
        txf[5, 10:11, r * 384:r * 384 + width] = r1d[r:r + 1, 0:width].astype(F32)
    gather_points([5])
    fill(5, 0)
    consts[2].wait()

    def apply(x):
        rhs = z[...].reshape(672, 768)
        o[x] = sum(dot(kv[s, x], rhs) for s in range(SPLITS))

    def per_element(values):
        return [values[e // 5:e // 5 + 1, e % 5:e % 5 + 1] for e in range(10)]

    lams = per_element(lam_ref[0].astype(F32))
    mus = per_element(mu_ref[0].astype(F32))
    cells = per_element(cell_ref[0])
    lam_rows = [halves(lams[a], lams[b]) for a, b in PAIRS]
    mu_rows = [halves(mus[a], mus[b]) for a, b in PAIRS]
    lam_point = sum(jnp.where(lane == e, lams[e], 0.0) for e in range(10))
    mu_point = sum(jnp.where(lane == e, mus[e], 0.0) for e in range(10))
    sel_row = lax.broadcasted_iota(jnp.int32, (128, 128), 0)
    direction = jnp.concatenate([dir_ref[...], dir_ref[...]], axis=1)
    choose = jnp.concatenate(
        [
            jnp.where(
                (sel_row == halves(a, b)) & (direction == halves(cells[a], cells[b])), 1.0, 0.0
            ).astype(BF16)
            for a, b in PAIRS
        ],
        axis=1,
    )

    first_row = lax.broadcasted_iota(jnp.int32, (8, 128), 0) == 0

    def merged(pieces):
        low, high = [functools.reduce(jnp.add, p) if p else 0.0 for p in pieces]
        return halves(low, high)

    def assemble(x):
        tile5 = o[x, 112:224, lane_tile(5)]
        cf[0:112, lane_tile(5)] = lam_point * o[x, 0:112, lane_tile(5)] + mu_point * tile5
        point = jnp.concatenate([cf[6 * m:6 * m + 8, lane_tile(5)] for m in range(18)], axis=1)
        point_hi = point.astype(BF16).astype(F32)
        fpb[x] = jnp.concatenate([point_hi, point - point_hi], axis=0).astype(BF16)
        k_hi, k_lo = hi_lo(tile5)
        source = dot(k_hi, choose) + dot(k_lo, choose)
        for i in range(5):
            cf[0:112, lane_tile(i)] = (
                lam_rows[i] * o[x, 0:112, lane_tile(i)]
                + mu_rows[i] * o[x, 112:224, lane_tile(i)]
                + source[:, lane_tile(i)]
            )
        fs[x, 8:16, :] = jnp.zeros((8, WIDE), F32)
        for ey in range(2):
            for t in range(39):
                stay, move = ([], []), ([], [])
                for h in range(2):
                    kc = 2 * t + h
                    ez, m = kc // 15, kc % 15
                    for ez_at, m_at in ((ez, m), (ez - 1, m + 15)):
                        if 0 <= ez_at < EZ and m_at < 18:
                            e = ey * 5 + ez_at
                            i = next(n for n, p in enumerate(PAIRS) if e in p)
                            half = PAIRS[i].index(e)
                            piece = cf[6 * m_at:6 * m_at + 8, lane_tile(i)]
                            (stay if half == h else move)[half].append(piece)
                total = merged(stay)
                if move[0] or move[1]:
                    total = total + pltpu.roll(merged(move), 64, 1)
                if ey == 0:
                    fs[x, 0:8, lane_tile(t)] = total
                else:
                    shared = jnp.where(first_row, fs[x, 5:13, lane_tile(t)], 0.0)
                    fs[x, 5:13, lane_tile(t)] = shared + total

    def place_point(x, values):
        values = values[0:8] + values[8:16]
        fs[x, 0:8, COLS:] = values[:, 0:128]
        shared = jnp.where(first_row, fs[x, 5:13, COLS:], 0.0)
        fs[x, 5:13, COLS:] = shared + values[:, 128:256]

    def pack_row(buffer, values):
        for r in range(-(-values.shape[1] // 384)):
            width = min(384, values.shape[1] - r * 384)
            buffer[r:r + 1, 0:width] = values[:, r * 384:r * 384 + width].astype(BF16)

    s2d[...] = jnp.zeros_like(s2d)
    s2y[...] = jnp.zeros_like(s2y)
    s2p[...] = jnp.zeros_like(s2p)
    apply(5)
    consts[3].wait()
    assemble(5)
    apply(0)
    place_point(5, dot(fpb[5], qv[...]))
    s2x[...] = fs[5].astype(BF16)
    pack_row(s2d, fs[5, 10:11, :])
    start(second[0])
    start(second[1])
    for x in range(5):
        if x < 4:
            apply(x + 1)
        assemble(x)
        pack_row(s2y.at[x], fs[x, 10:11, 0:COLS])
        start(second[3 + x])
    points = dot(fpb[0:5].reshape(80, 18 * 128), qv[...])
    for x in range(5):
        place_point(x, points[16 * x:16 * x + 16])
        s2p[x:x + 1, :] = fs[x, 10:11, COLS:].astype(BF16)
    start(second[2])

    def add_row(x, buffer, width):
        for r in range(-(-width // 384)):
            size = min(384, width - r * 384)
            cols = slice(r * 384, r * 384 + size)
            fs[x, 0:1, cols] = fs[x, 0:1, cols] + buffer[r:r + 1, 0:size].astype(F32)

    def finish(x, carry):
        rows = pl.ds(pl.multiple_of(x * 16, 16), 16)
        for pair in range(13):
            parts = []
            for t in range(3 * pair, 3 * pair + 3):
                cols = lane_tile(t)
                full = 2.0 * txf[x, :, cols] - tpf[x, :, cols] - wf[x, 0:16, cols] * fs[x, :, cols]
                tan_out[x, :, cols] = full[0:10].astype(BF16)
                parts.append(full * wf[x, 16:32, cols])
            a, b, c = parts
            amount = halves(a + pltpu.roll(a, 64, 1), c + pltpu.roll(c, 64, 1)) + b
            high, low = hi_lo(amount)
            uu[pair, rows, 0:128] = high
            uu[pair, rows, 128:256] = low
        return carry

    def finish_points(x, carry):
        fs[x, 0:1, COLS:] = fs[x, 0:1, COLS:] + r2p[x:x + 1, :].astype(F32)
        scale = exf[x, 0:16].astype(F32) + exf[x, 16:32].astype(F32)
        moved = (
            2.0 * txf[x, :, COLS:]
            - prep[1, x]
            + scale * (prep[2, x] - fs[x, :, COLS:])
        )
        disp_out[x] = moved.astype(BF16)
        return carry

    outs = [
        pltpu.make_async_copy(tan_out.at[x], tan_hbm_out.at[x], out_sem.at[x]) for x in range(5)
    ]
    for x in (1, 2, 3):
        arrived(second[3 + x])
        add_row(x, r2y.at[x], COLS)
    lax.fori_loop(1, 4, finish, 0)
    for x in (1, 2, 3):
        outs[x].start()
    arrived(second[0])
    arrived(second[1])
    arrived(second[3])
    fs[0] = fs[0] + r2x[...].astype(F32)
    add_row(0, r2y.at[0], COLS)
    add_row(0, r2d, WIDE)
    finish(0, 0)
    outs[0].start()
    arrived(second[7])
    add_row(4, r2y.at[4], COLS)
    finish(4, 0)
    outs[4].start()

    per_row = PORTS // ny
    slot = gx * nsrc_y + (gy - first_src)

    def port_copy(target_x, target_y, slot_at):
        return pltpu.make_async_remote_copy(
            src_ref=pbuf.at[target_y], dst_ref=prec.at[slot_at],
            send_sem=psend.at[target_x * ny + target_y], recv_sem=precv.at[slot_at],
            device_id=(target_x, target_y), device_id_type=MESH,
        )

    @pl.when(is_src)
    def _():
        square = dot(oht[...], uu[...].reshape(1040, 256))
        square = square[:, 0:128] + square[:, 128:256]
        amp = square[0:64] + pltpu.roll(square[64:128], 64, 1)
        for g in range(ny):
            pbuf[g] = jnp.zeros((8, 128), F32)
            pbuf[g, 0:per_row, :] = amp[g * per_row:(g + 1) * per_row]

        def send(t, carry):
            @pl.when(t != me)
            def _():
                port_copy(t // ny, t % ny, slot).start()
            return carry

        lax.fori_loop(0, n_all, send, 0)
        prec[slot] = pbuf[gy]

    arrived(second[2])
    for x in range(5):
        finish_points(x, 0)

    def collect(s, acc):
        @pl.when(jnp.logical_or(jnp.logical_not(is_src), s != slot))
        def _():
            port_copy(gx, gy, s).wait_recv()
        return acc + prec[s]

    acc = lax.fori_loop(0, nx * nsrc_y, collect, jnp.zeros((8, 128), F32))
    per_col = NT // nx
    mine = acc[0:per_row, 0:per_col]
    for h in range(1, nx):
        mine = jnp.where(gx == h, acc[0:per_row, h * per_col:(h + 1) * per_col], mine)
    port_out[...] = mine

    for copy in outs:
        copy.wait()
    for item in first + second:
        sent(item)

    @pl.when(is_src)
    def _():
        def drain(t, carry):
            @pl.when(t != me)
            def _():
                port_copy(t // ny, t % ny, slot).wait_send()
            return carry

        lax.fori_loop(0, n_all, drain, 0)


def settle(tan, port, point, tan_out, port_out, point_out):
    tan_out[...] = tan[...]
    port_out[...] = port[...]
    for c in range(3):
        point_out[0, :, c, :] = point[0, 0:10, 32 * c:32 * c + NZN]


def per_device(
    nx, ny,
    disp, disp_prev, tangent, tangent_prev, lame_lambda, lame_mu, node_mass, force,
    cell_block, direction_block, port_id, port_mode,
):
    rows = disp.shape[1]
    nsrc_y = -(-PORT_DEPTH // rows)
    primal = [a.transpose(0, 1, 3, 2) for a in (disp, disp_prev, force, port_mode)]
    expand, gather, scatter = layout_tables()
    tables = element_tables()
    nsrc = nx * nsrc_y
    vmem = pl.BlockSpec(memory_space=pltpu.VMEM)
    hbm = pl.BlockSpec(memory_space=pl.ANY)
    big = pltpu.VMEM((16, WIDE), BF16)
    small = pltpu.VMEM((16, 384), BF16)
    packed = pltpu.VMEM((16, 3200), BF16)
    rows5 = pltpu.VMEM((5, 16, 384), BF16)
    point = pltpu.VMEM((16, 128), BF16)
    tangent_next, moved, port_amp = pl.pallas_call(
        functools.partial(kernel, nx, ny, nsrc_y),
        out_shape=(
            jax.ShapeDtypeStruct(tangent.shape, BF16),
            jax.ShapeDtypeStruct((5, 16, 128), BF16),
            jax.ShapeDtypeStruct((PORTS // ny, NT // nx), F32),
        ),
        in_specs=[vmem] * 4 + [hbm] * 2 + [vmem] * 6 + [hbm] * 4,
        out_specs=(hbm, vmem, vmem),
        scratch_shapes=[
            pltpu.VMEM(tangent.shape, BF16),
            pltpu.VMEM(tangent.shape, BF16),
            pltpu.VMEM(tangent.shape, BF16),
            pltpu.SemaphoreType.DMA((5,)),
            pltpu.VMEM((4, 5, 16, 128), F32),
            pltpu.VMEM(tables.shape, BF16),
            pltpu.VMEM(expand.shape, BF16),
            pltpu.VMEM(gather.shape, BF16),
            pltpu.VMEM(scatter.shape, BF16),
            pltpu.SemaphoreType.DMA((6,)),
            pltpu.VMEM((6, 16, WIDE), F32),
            pltpu.VMEM((5, 16, COLS), F32),
            pltpu.VMEM((5, 48, 128), BF16),
            pltpu.VMEM((5, 32, COLS), F32),
            pltpu.VMEM((13, 80, 128), F32),
            pltpu.VMEM((128, 1040), BF16),
            pltpu.VMEM((13, 80, 256), BF16),
            pltpu.VMEM((16, 128), F32),
            pltpu.VMEM((16, 128), jnp.int32),
            pltpu.VMEM((6, 8, 18 * 128), F32),
            pltpu.VMEM((6, 112, 768), BF16),
            pltpu.VMEM((6, 224, 768), F32),
            pltpu.VMEM((112, 768), F32),
            pltpu.VMEM((112, 768), F32),
            pltpu.VMEM((6, 16, WIDE), F32),
            pltpu.VMEM((6, 16, 18 * 128), BF16),
            packed, big, small, packed, big, small,
            big, rows5, small, point, big, rows5, small, point,
            pltpu.VMEM((ny, 8, 128), F32),
            pltpu.VMEM((nsrc, 8, 128), F32),
            pltpu.SemaphoreType.DMA((11,)),
            pltpu.SemaphoreType.DMA((11,)),
            pltpu.SemaphoreType.DMA((nx * ny,)),
            pltpu.SemaphoreType.DMA((nsrc,)),
        ],
        compiler_params=pltpu.CompilerParams(
            collective_id=0, has_side_effects=True, vmem_limit_bytes=56 * 1024 * 1024
        ),
    )(
        lame_lambda, lame_mu, cell_block, direction_block[None], tangent, tangent_prev, *primal, node_mass, port_id,
        jnp.asarray(tables), jnp.asarray(expand), jnp.asarray(gather), jnp.asarray(scatter),
    )
    layer = pl.BlockSpec((1,) + tangent.shape[1:], lambda x: (x, 0, 0))
    whole = pl.BlockSpec(port_amp.shape, lambda x: (0, 0))
    points = pl.BlockSpec((1,) + primal[0].shape[1:], lambda x: (x, 0, 0, 0))
    tangent_next, port_amp, moved = pl.pallas_call(
        settle,
        grid=(5,),
        out_shape=(
            jax.ShapeDtypeStruct(tangent_next.shape, BF16),
            jax.ShapeDtypeStruct(port_amp.shape, F32),
            jax.ShapeDtypeStruct(primal[0].shape, BF16),
        ),
        in_specs=[layer, whole, pl.BlockSpec((1, 16, 128), lambda x: (x, 0, 0))],
        out_specs=(layer, whole, points),
    )(tangent_next, port_amp, moved)
    moved = moved.transpose(0, 1, 3, 2)
    return moved, tangent_next, port_amp


def solution(mesh):
    nx, ny = mesh.shape["gx"], mesh.shape["gy"]
    return jax.shard_map(
        functools.partial(per_device, nx, ny),
        mesh=mesh,
        in_specs=(
            P("gx", "gy", None, None),
            P("gx", "gy", None, None),
            P("gx", "gy", None),
            P("gx", "gy", None),
            P("gx", "gy", None),
            P("gx", "gy", None),
            P("gx", "gy", None),
            P("gx", "gy", None, None),
            P("gx", "gy", None),
            P(),
            P("gx", "gy", None),
            P("gx", "gy", None, None),
        ),
        out_specs=(P("gx", "gy", None, None), P("gx", "gy", None), P("gy", "gx")),
        check_vma=False,
    )
```

```python
import functools

import jax
import jax.numpy as jnp
import numpy as np
from jax import lax
from jax.experimental import pallas as pl
from jax.experimental.pallas import tpu as pltpu
from jax.sharding import PartitionSpec as P

PORTS = 64
PORT_DEPTH = 40
EZ = 5
NT = 64
NZN = 26
GLL_POINTS = np.array(
    [-1.0, -0.765055323929465, -0.285231516480645, 0.285231516480645, 0.765055323929465, 1.0]
)
GLL_WEIGHTS = np.array(
    [
        1.0 / 15.0,
        0.378474956297847,
        0.554858377035486,
        0.554858377035486,
        0.378474956297847,
        1.0 / 15.0,
    ]
)
STEP_SQUARED = 0.03
MESH = pl.DeviceIdType.MESH
F32 = jnp.float32
BF16 = jnp.bfloat16
COLS = 3 * NZN * NT
WIDE = COLS + 128
PAIRS = ((0, 1), (2, 3), (5, 6), (7, 8), (4, 9))


def derivative_table():
    identity = np.eye(6)
    differences = GLL_POINTS[:, None] - GLL_POINTS[None, :] + identity
    barycentric = 1.0 / np.prod(differences, axis=1)
    matrix = barycentric[None, :] / barycentric[:, None] / differences
    matrix = matrix * (1.0 - identity)
    matrix = matrix - identity * matrix.sum(axis=1)[:, None]
    return matrix


def split_bf16(table):
    high = table.astype(jnp.bfloat16)
    low = (table - high.astype(np.float64)).astype(jnp.bfloat16)
    return [high, low]


def element_tables():
    d = derivative_table()
    eye = np.eye(6)
    ds = [
        np.kron(np.kron(d, eye), eye),
        np.kron(np.kron(eye, d), eye),
        np.kron(np.kron(eye, eye), d),
    ]
    w = np.kron(np.kron(GLL_WEIGHTS, GLL_WEIGHTS), GLL_WEIGHTS)[:, None]
    lap = sum(m.T @ (w * m) for m in ds)
    both = np.zeros((2, 216, 3, 216, 3))
    for c in range(3):
        for e in range(3):
            both[0, :, c, :, e] = ds[c].T @ (w * ds[e])
            both[1, :, c, :, e] = ds[e].T @ (w * ds[c]) + (lap if c == e else 0.0)
    both = both.reshape(2, 6, 6, 6, 3, 6, 6, 6, 3)
    both = both.transpose(0, 1, 3, 4, 2, 5, 7, 8, 6)
    both = both.reshape(2, 6, 108, 6, 108)
    both = np.pad(both, ((0, 0), (0, 0), (0, 4), (0, 0), (0, 4))).reshape(2, 6, 112, 672)
    both = both.transpose(1, 0, 2, 3).reshape(6, 224, 672)
    return np.concatenate(split_bf16(both), axis=1)


def layout_tables():
    expand = np.zeros((128, NZN, 3, NT))
    for k in range(NZN):
        for c in range(3):
            expand[c * 32 + k, k, c, :] = 1.0
    gather = np.zeros((2, 128, 18, 128))
    for ey in range(2):
        for ez in range(EZ):
            for kz in range(6):
                for c in range(3):
                    gather[ey, c * 32 + 5 * ez + kz, kz * 3 + c, ey * 5 + ez] = 1.0
    gather = gather.reshape(256, 18 * 128)
    return (
        expand.reshape(128, COLS).astype(jnp.bfloat16),
        gather.astype(jnp.bfloat16),
        np.ascontiguousarray(gather.T).astype(jnp.bfloat16),
    )


X_PACK = (
    (np.s_[0:10, 0:3200], np.s_[0:10, 0:3200]),
    (np.s_[10:16, 0:1920], np.s_[0:6, 3200:5120]),
    (np.s_[10:14, 1920:3200], np.s_[6:10, 3200:4480]),
    (np.s_[14:16, 1920:2560], np.s_[6:8, 4480:5120]),
    (np.s_[14:16, 2560:3200], np.s_[8:10, 4480:5120]),
)


def lane_tile(t):
    return slice(t * 128, (t + 1) * 128)


def hi_lo(values):
    high = values.astype(BF16)
    return high, (values - high.astype(F32)).astype(BF16)


def dot(a, b):
    return jnp.dot(a, b, preferred_element_type=F32)


def kernel(
    nx, ny, nsrc_y,
    lam_ref, mu_ref, cell_ref, dir_ref, tan_hbm, tanp_hbm, now, past, load, mode, mass, pid, k_hbm, e_hbm, p_hbm, q_hbm,
    tan_hbm_out, disp_out, port_out,
    tan, tanp, tan_out, out_sem, prep,
    kv, ev, pv, qv, const_sem,
    txf, tpf, exf, wf, oh, oht, uu, ms, ps, dsc, z, o, zf, cf, fs, fpb,
    s1x, s1y, s1d, r1x, r1y, r1d, s2x, s2y, s2d, s2p, r2x, r2y, r2d, r2p,
    pbuf, prec, send_sem, recv_sem, psend, precv,
):
    gx = lax.axis_index("gx")
    gy = lax.axis_index("gy")
    consts = [
        pltpu.make_async_copy(a, b, const_sem.at[i])
        for i, (a, b) in enumerate(
            (
                (e_hbm, ev), (p_hbm, pv), (k_hbm, kv), (q_hbm, qv),
                (tan_hbm, tan), (tanp_hbm, tanp),
            )
        )
    ]
    for i in (4, 5, 0, 1, 2, 3):
        consts[i].start()

    x_lo, x_hi = gx > 0, gx < nx - 1
    y_lo, y_hi = gy > 0, gy < ny - 1
    first_src = ny - nsrc_y
    is_src = gy >= first_src
    n_all = nx * ny
    me = gx * ny + gy

    barrier = pltpu.get_barrier_semaphore()
    around = (
        (x_lo, -1, 0), (x_hi, 1, 0), (y_lo, 0, -1), (y_hi, 0, 1),
        (jnp.logical_and(x_lo, y_lo), -1, -1), (jnp.logical_and(x_hi, y_hi), 1, 1),
    )
    expected = jnp.int32(0)
    for there, dx, dy in around:
        @pl.when(there)
        def _(dx=dx, dy=dy):
            pl.semaphore_signal(barrier, inc=1, device_id=(gx + dx, gy + dy), device_id_type=MESH)
        expected = expected + there.astype(jnp.int32)

    def greet(s, carry):
        sx = s // nsrc_y
        sy = first_src + s % nsrc_y

        @pl.when(sx * ny + sy != me)
        def _():
            pl.semaphore_signal(barrier, inc=1, device_id=(sx, sy), device_id_type=MESH)
        return carry

    lax.fori_loop(0, nx * nsrc_y, greet, 0)
    expected = expected + is_src.astype(jnp.int32) * (n_all - 1)

    def lanes(source, index, x):
        for c in range(3):
            prep[index, x, 0:10, 32 * c:32 * c + NZN] = source[x, :, c, :].astype(F32)

    prep[...] = jnp.zeros_like(prep)
    lanes(now, 0, 0)

    consts[4].wait()
    layer = jnp.concatenate([tan[0], prep[0, 0, 0:10, :].astype(BF16)], axis=1)
    for to, at in X_PACK:
        s1x[to] = layer[at]
    pl.semaphore_wait(barrier, expected)

    def remote(index, src, dst, dx, dy):
        return pltpu.make_async_remote_copy(
            src_ref=src, dst_ref=dst, send_sem=send_sem.at[index], recv_sem=recv_sem.at[index],
            device_id=(gx + dx, gy + dy), device_id_type=MESH,
        )

    first = (
        (remote(0, s1x, r1x, -1, 0), x_lo, x_hi, r1x),
        (remote(1, s1y, r1y, 0, -1), y_lo, y_hi, r1y),
        (remote(2, s1d, r1d, -1, -1), jnp.logical_and(x_lo, y_lo), jnp.logical_and(x_hi, y_hi), r1d),
    )
    second = (
        (remote(3, s2x, r2x, 1, 0), x_hi, x_lo, r2x),
        (remote(4, s2d, r2d, 1, 1), jnp.logical_and(x_hi, y_hi), jnp.logical_and(x_lo, y_lo), r2d),
        (remote(5, s2p, r2p, 0, 1), y_hi, y_lo, r2p),
    ) + tuple(
        (remote(6 + x, s2y.at[x], r2y.at[x], 0, 1), y_hi, y_lo, r2y.at[x]) for x in range(5)
    )

    def start(item):
        copy, sends, _, _ = item

        @pl.when(sends)
        def _():
            copy.start()

    def arrived(item):
        copy, _, receives, buffer = item

        @pl.when(receives)
        def _():
            copy.wait_recv()

        @pl.when(jnp.logical_not(receives))
        def _():
            buffer[...] = jnp.zeros_like(buffer)

    def sent(item):
        copy, sends, _, _ = item

        @pl.when(sends)
        def _():
            copy.wait_send()

    start(first[0])
    s1y[...] = jnp.zeros_like(s1y)
    s1d[...] = jnp.zeros_like(s1d)
    for x in range(5):
        if x > 0:
            lanes(now, 0, x)
        s1y[x:x + 1, 0:COLS] = tan[x, 0:1, :]
        s1y[x:x + 1, COLS:] = prep[0, x, 0:1, :].astype(BF16)
    row = s1y[0:1, :]
    for r in range(14):
        width = min(384, WIDE - r * 384)
        s1d[r:r + 1, 0:width] = row[:, r * 384:r * 384 + width]
    start(first[1])
    start(first[2])

    lane = lax.broadcasted_iota(jnp.int32, (1, 128), 1)
    low_half = lane < 64

    def halves(a, b):
        return jnp.where(low_half, a, b)

    def prepare(x, carry):
        txf[x, 8:16, :] = jnp.zeros((8, WIDE), F32)
        tpf[x, 8:16, :] = jnp.zeros((8, COLS), F32)
        txf[x, 0:10, 0:COLS] = tan[x].astype(F32)
        txf[x, :, COLS:] = prep[0, x]
        for index, source in ((1, past), (2, load), (3, mode)):
            lanes(source, index, x)
        tpf[x, 0:10, :] = tanp[x].astype(F32)
        ms[...] = jnp.ones_like(ms)
        ps[...] = jnp.full(ps.shape, PORTS, jnp.int32)
        ms[0:10, 0:NZN] = mass[x]
        ps[0:10, 0:NZN] = pid[x]
        rep_row = lax.broadcasted_iota(jnp.int32, (128, 128), 0)
        rep_col = lax.broadcasted_iota(jnp.int32, (128, 128), 1)
        rep = jnp.where((rep_col % 32 == rep_row) & (rep_row < NZN), 1.0, 0.0).astype(BF16)
        inv_hi, inv_lo = hi_lo(STEP_SQUARED / ms[...])
        exf[x, 0:16] = dot(inv_hi, rep).astype(BF16)
        exf[x, 16:32] = dot(inv_lo, rep).astype(BF16)
        exf[x, 32:48] = prep[3, x].astype(BF16)
        ids = ps[...]
        rows = pl.ds(pl.multiple_of(x * 16, 16), 16)
        for pair in range(13):
            port = halves(ids[:, 2 * pair:2 * pair + 1], ids[:, 2 * pair + 1:2 * pair + 2])
            oh[pair, rows, :] = jnp.where(port == lane % 64, 1.0, 0.0)
        return carry

    consts[5].wait()
    lax.fori_loop(0, 5, prepare, 0)

    @pl.when(is_src)
    def _():
        oht[...] = oh[...].reshape(1040, 128).T.astype(BF16)

    consts[0].wait()
    lhs = exf[...].reshape(240, 128)

    def widen(n, carry):
        cols = pl.ds(pl.multiple_of(n * 384, 384), 384)
        w = dot(lhs, ev[:, cols]).reshape(5, 48, 384)
        wf[:, 0:16, cols] = w[:, 0:16] + w[:, 16:32]
        wf[:, 16:32, cols] = w[:, 32:48]
        return carry

    lax.fori_loop(0, COLS // 384, widen, 0)

    def gather_points(layers):
        near = jnp.concatenate([txf[x, 0:8, COLS:] for x in layers], axis=0)
        far = jnp.concatenate([txf[x, 5:13, COLS:] for x in layers], axis=0)
        gathered = dot(jnp.concatenate([near, far], axis=1).astype(BF16), pv[...])
        for n, x in enumerate(layers):
            dsc[x] = gathered[8 * n:8 * n + 8]

    arrived(first[1])
    for x in range(5):
        txf[x, 10:11, :] = r1y[x:x + 1, :].astype(F32)
    consts[1].wait()
    gather_points(range(5))

    zf[96:112, :] = jnp.zeros((16, 768), F32)

    def fill(x, carry):
        def tile(m, ey, ez):
            kc = 15 * ez + m
            return txf[x, 5 * ey:5 * ey + 8, lane_tile(kc // 2)]

        for m in range(18):
            rows = slice(6 * m, 6 * m + 8)
            for i, (e1, e2) in enumerate(PAIRS):
                a, b = tile(m, e1 // 5, e1 % 5), tile(m, e2 // 5, e2 % 5)
                a_half, b_half = (15 * (e1 % 5) + m) % 2, (15 * (e2 % 5) + m) % 2
                if a_half == 0 and b_half == 1:
                    both = halves(a, b)
                elif a_half == 1 and b_half == 0:
                    both = pltpu.roll(halves(b, a), 64, 1)
                elif a_half == 0:
                    both = halves(a, pltpu.roll(b, 64, 1))
                else:
                    both = halves(pltpu.roll(a, 64, 1), b)
                zf[rows, lane_tile(i)] = both
            zf[rows, lane_tile(5)] = dsc[x, :, lane_tile(m)]
        z[x] = zf[...].astype(BF16)
        return carry

    lax.fori_loop(0, 5, fill, 0)
    arrived(first[0])
    arrived(first[2])
    txf[5, 8:16, :] = jnp.zeros((8, WIDE), F32)
    for to, at in X_PACK:
        txf[(5,) + at] = r1x[to].astype(F32)
    for r in range(14):
        width = min(384, WIDE - r * 384)
        txf[5, 10:11, r * 384:r * 384 + width] = r1d[r:r + 1, 0:width].astype(F32)
    gather_points([5])
    fill(5, 0)
    consts[2].wait()

    def apply(x):
        rhs = z[...].reshape(672, 768)
        full = dot(kv[x], rhs)
        o[x] = full[0:224] + full[224:448]

    def per_element(values):
        return [values[e // 5:e // 5 + 1, e % 5:e % 5 + 1] for e in range(10)]

    lams = per_element(lam_ref[0].astype(F32))
    mus = per_element(mu_ref[0].astype(F32))
    cells = per_element(cell_ref[0])
    lam_rows = [halves(lams[a], lams[b]) for a, b in PAIRS]
    mu_rows = [halves(mus[a], mus[b]) for a, b in PAIRS]
    lam_point = sum(jnp.where(lane == e, lams[e], 0.0) for e in range(10))
    mu_point = sum(jnp.where(lane == e, mus[e], 0.0) for e in range(10))
    sel_row = lax.broadcasted_iota(jnp.int32, (128, 128), 0)
    direction = jnp.concatenate([dir_ref[...], dir_ref[...]], axis=1)
    choose = jnp.concatenate(
        [
            jnp.where(
                (sel_row == halves(a, b)) & (direction == halves(cells[a], cells[b])), 1.0, 0.0
            ).astype(BF16)
            for a, b in PAIRS
        ],
        axis=1,
    )

    first_row = lax.broadcasted_iota(jnp.int32, (8, 128), 0) == 0

    def merged(pieces):
        low, high = [functools.reduce(jnp.add, p) if p else 0.0 for p in pieces]
        return halves(low, high)

    def assemble(x):
        tile5 = o[x, 112:224, lane_tile(5)]
        cf[0:112, lane_tile(5)] = lam_point * o[x, 0:112, lane_tile(5)] + mu_point * tile5
        point = jnp.concatenate([cf[6 * m:6 * m + 8, lane_tile(5)] for m in range(18)], axis=1)
        point_hi = point.astype(BF16).astype(F32)
        fpb[x] = jnp.concatenate([point_hi, point - point_hi], axis=0).astype(BF16)
        k_hi, k_lo = hi_lo(tile5)
        source = dot(k_hi, choose) + dot(k_lo, choose)
        for i in range(5):
            cf[0:112, lane_tile(i)] = (
                lam_rows[i] * o[x, 0:112, lane_tile(i)]
                + mu_rows[i] * o[x, 112:224, lane_tile(i)]
                + source[:, lane_tile(i)]
            )
        fs[x, 8:16, :] = jnp.zeros((8, WIDE), F32)
        for ey in range(2):
            for t in range(39):
                stay, move = ([], []), ([], [])
                for h in range(2):
                    kc = 2 * t + h
                    ez, m = kc // 15, kc % 15
                    for ez_at, m_at in ((ez, m), (ez - 1, m + 15)):
                        if 0 <= ez_at < EZ and m_at < 18:
                            e = ey * 5 + ez_at
                            i = next(n for n, p in enumerate(PAIRS) if e in p)
                            half = PAIRS[i].index(e)
                            piece = cf[6 * m_at:6 * m_at + 8, lane_tile(i)]
                            (stay if half == h else move)[half].append(piece)
                total = merged(stay)
                if move[0] or move[1]:
                    total = total + pltpu.roll(merged(move), 64, 1)
                if ey == 0:
                    fs[x, 0:8, lane_tile(t)] = total
                else:
                    shared = jnp.where(first_row, fs[x, 5:13, lane_tile(t)], 0.0)
                    fs[x, 5:13, lane_tile(t)] = shared + total

    def place_point(x, values):
        values = values[0:8] + values[8:16]
        fs[x, 0:8, COLS:] = values[:, 0:128]
        shared = jnp.where(first_row, fs[x, 5:13, COLS:], 0.0)
        fs[x, 5:13, COLS:] = shared + values[:, 128:256]

    def pack_row(buffer, values):
        for r in range(-(-values.shape[1] // 384)):
            width = min(384, values.shape[1] - r * 384)
            buffer[r:r + 1, 0:width] = values[:, r * 384:r * 384 + width].astype(BF16)

    s2d[...] = jnp.zeros_like(s2d)
    s2y[...] = jnp.zeros_like(s2y)
    s2p[...] = jnp.zeros_like(s2p)
    apply(5)
    consts[3].wait()
    assemble(5)
    apply(0)
    place_point(5, dot(fpb[5], qv[...]))
    s2x[...] = fs[5].astype(BF16)
    pack_row(s2d, fs[5, 10:11, :])
    start(second[0])
    start(second[1])
    for x in range(5):
        if x < 4:
            apply(x + 1)
        assemble(x)
        pack_row(s2y.at[x], fs[x, 10:11, 0:COLS])
        start(second[3 + x])
    points = dot(fpb[0:5].reshape(80, 18 * 128), qv[...])
    for x in range(5):
        place_point(x, points[16 * x:16 * x + 16])
        s2p[x:x + 1, :] = fs[x, 10:11, COLS:].astype(BF16)
    start(second[2])

    def add_row(x, buffer, width):
        for r in range(-(-width // 384)):
            size = min(384, width - r * 384)
            cols = slice(r * 384, r * 384 + size)
            fs[x, 0:1, cols] = fs[x, 0:1, cols] + buffer[r:r + 1, 0:size].astype(F32)

    def finish(x, carry):
        rows = pl.ds(pl.multiple_of(x * 16, 16), 16)
        for pair in range(13):
            parts = []
            for t in range(3 * pair, 3 * pair + 3):
                cols = lane_tile(t)
                full = 2.0 * txf[x, :, cols] - tpf[x, :, cols] - wf[x, 0:16, cols] * fs[x, :, cols]
                tan_out[x, :, cols] = full[0:10].astype(BF16)
                parts.append(full * wf[x, 16:32, cols])
            a, b, c = parts
            amount = halves(a + pltpu.roll(a, 64, 1), c + pltpu.roll(c, 64, 1)) + b
            high, low = hi_lo(amount)
            uu[pair, rows, 0:128] = high
            uu[pair, rows, 128:256] = low
        return carry

    def finish_points(x, carry):
        fs[x, 0:1, COLS:] = fs[x, 0:1, COLS:] + r2p[x:x + 1, :].astype(F32)
        scale = exf[x, 0:16].astype(F32) + exf[x, 16:32].astype(F32)
        moved = (
            2.0 * txf[x, :, COLS:]
            - prep[1, x]
            + scale * (prep[2, x] - fs[x, :, COLS:])
        )
        for c in range(3):
            disp_out[x, :, c, :] = moved[0:10, 32 * c:32 * c + NZN].astype(BF16)
        return carry

    outs = [
        pltpu.make_async_copy(tan_out.at[x], tan_hbm_out.at[x], out_sem.at[x]) for x in range(5)
    ]
    for x in (1, 2, 3):
        arrived(second[3 + x])
        add_row(x, r2y.at[x], COLS)
    lax.fori_loop(1, 4, finish, 0)
    for x in (1, 2, 3):
        outs[x].start()
    arrived(second[0])
    arrived(second[1])
    arrived(second[3])
    fs[0] = fs[0] + r2x[...].astype(F32)
    add_row(0, r2y.at[0], COLS)
    add_row(0, r2d, WIDE)
    finish(0, 0)
    outs[0].start()
    arrived(second[7])
    add_row(4, r2y.at[4], COLS)
    finish(4, 0)
    outs[4].start()

    per_row = PORTS // ny
    slot = gx * nsrc_y + (gy - first_src)

    def port_copy(target_x, target_y, slot_at):
        return pltpu.make_async_remote_copy(
            src_ref=pbuf.at[target_y], dst_ref=prec.at[slot_at],
            send_sem=psend.at[target_x * ny + target_y], recv_sem=precv.at[slot_at],
            device_id=(target_x, target_y), device_id_type=MESH,
        )

    @pl.when(is_src)
    def _():
        square = dot(oht[...], uu[...].reshape(1040, 256))
        square = square[:, 0:128] + square[:, 128:256]
        amp = square[0:64] + pltpu.roll(square[64:128], 64, 1)
        for g in range(ny):
            pbuf[g] = jnp.zeros((8, 128), F32)
            pbuf[g, 0:per_row, :] = amp[g * per_row:(g + 1) * per_row]

        def send(t, carry):
            @pl.when(t != me)
            def _():
                port_copy(t // ny, t % ny, slot).start()
            return carry

        lax.fori_loop(0, n_all, send, 0)
        prec[slot] = pbuf[gy]

    arrived(second[2])
    for x in range(5):
        finish_points(x, 0)

    def collect(s, acc):
        @pl.when(jnp.logical_or(jnp.logical_not(is_src), s != slot))
        def _():
            port_copy(gx, gy, s).wait_recv()
        return acc + prec[s]

    acc = lax.fori_loop(0, nx * nsrc_y, collect, jnp.zeros((8, 128), F32))
    per_col = NT // nx
    mine = acc[0:per_row, 0:per_col]
    for h in range(1, nx):
        mine = jnp.where(gx == h, acc[0:per_row, h * per_col:(h + 1) * per_col], mine)
    port_out[...] = mine

    for copy in outs:
        copy.wait()
    for item in first + second:
        sent(item)

    @pl.when(is_src)
    def _():
        def drain(t, carry):
            @pl.when(t != me)
            def _():
                port_copy(t // ny, t % ny, slot).wait_send()
            return carry

        lax.fori_loop(0, n_all, drain, 0)


def settle(tan, port, point, tan_out, port_out, point_out, held, sem_in, sem_out):
    layers = range(held.shape[0])
    into = [pltpu.make_async_copy(tan.at[x], held.at[x], sem_in.at[x]) for x in layers]
    out = [pltpu.make_async_copy(held.at[x], tan_out.at[x], sem_out.at[x]) for x in layers]
    for copy in into:
        copy.start()
    port_out[...] = port[...]
    point_out[...] = point[...]
    for x in layers:
        into[x].wait()
        out[x].start()
    for copy in out:
        copy.wait()


def per_device(
    nx, ny,
    disp, disp_prev, tangent, tangent_prev, lame_lambda, lame_mu, node_mass, force,
    cell_block, direction_block, port_id, port_mode,
):
    rows = disp.shape[1]
    nsrc_y = -(-PORT_DEPTH // rows)
    primal = [a.transpose(0, 1, 3, 2) for a in (disp, disp_prev, force, port_mode)]
    expand, gather, scatter = layout_tables()
    tables = element_tables()
    nsrc = nx * nsrc_y
    vmem = pl.BlockSpec(memory_space=pltpu.VMEM)
    hbm = pl.BlockSpec(memory_space=pl.ANY)
    big = pltpu.VMEM((16, WIDE), BF16)
    small = pltpu.VMEM((16, 384), BF16)
    packed = pltpu.VMEM((16, 3200), BF16)
    rows5 = pltpu.VMEM((5, 16, 384), BF16)
    point = pltpu.VMEM((16, 128), BF16)
    tangent_next, moved, port_amp = pl.pallas_call(
        functools.partial(kernel, nx, ny, nsrc_y),
        out_shape=(
            jax.ShapeDtypeStruct(tangent.shape, BF16),
            jax.ShapeDtypeStruct(primal[0].shape, BF16),
            jax.ShapeDtypeStruct((PORTS // ny, NT // nx), F32),
        ),
        in_specs=[vmem] * 4 + [hbm] * 2 + [vmem] * 6 + [hbm] * 4,
        out_specs=(hbm, vmem, vmem),
        scratch_shapes=[
            pltpu.VMEM(tangent.shape, BF16),
            pltpu.VMEM(tangent.shape, BF16),
            pltpu.VMEM(tangent.shape, BF16),
            pltpu.SemaphoreType.DMA((5,)),
            pltpu.VMEM((4, 5, 16, 128), F32),
            pltpu.VMEM(tables.shape, BF16),
            pltpu.VMEM(expand.shape, BF16),
            pltpu.VMEM(gather.shape, BF16),
            pltpu.VMEM(scatter.shape, BF16),
            pltpu.SemaphoreType.DMA((6,)),
            pltpu.VMEM((6, 16, WIDE), F32),
            pltpu.VMEM((5, 16, COLS), F32),
            pltpu.VMEM((5, 48, 128), BF16),
            pltpu.VMEM((5, 32, COLS), F32),
            pltpu.VMEM((13, 80, 128), F32),
            pltpu.VMEM((128, 1040), BF16),
            pltpu.VMEM((13, 80, 256), BF16),
            pltpu.VMEM((16, 128), F32),
            pltpu.VMEM((16, 128), jnp.int32),
            pltpu.VMEM((6, 8, 18 * 128), F32),
            pltpu.VMEM((6, 112, 768), BF16),
            pltpu.VMEM((6, 224, 768), F32),
            pltpu.VMEM((112, 768), F32),
            pltpu.VMEM((112, 768), F32),
            pltpu.VMEM((6, 16, WIDE), F32),
            pltpu.VMEM((6, 16, 18 * 128), BF16),
            packed, big, small, packed, big, small,
            big, rows5, small, point, big, rows5, small, point,
            pltpu.VMEM((ny, 8, 128), F32),
            pltpu.VMEM((nsrc, 8, 128), F32),
            pltpu.SemaphoreType.DMA((11,)),
            pltpu.SemaphoreType.DMA((11,)),
            pltpu.SemaphoreType.DMA((nx * ny,)),
            pltpu.SemaphoreType.DMA((nsrc,)),
        ],
        compiler_params=pltpu.CompilerParams(
            collective_id=0, has_side_effects=True, vmem_limit_bytes=56 * 1024 * 1024
        ),
    )(
        lame_lambda, lame_mu, cell_block, direction_block[None], tangent, tangent_prev, *primal, node_mass, port_id,
        jnp.asarray(tables), jnp.asarray(expand), jnp.asarray(gather), jnp.asarray(scatter),
    )
    tangent_next, port_amp, moved = pl.pallas_call(
        settle,
        out_shape=(
            jax.ShapeDtypeStruct(tangent_next.shape, BF16),
            jax.ShapeDtypeStruct(port_amp.shape, F32),
            jax.ShapeDtypeStruct(moved.shape, BF16),
        ),
        in_specs=[hbm, vmem, vmem],
        out_specs=(hbm, vmem, vmem),
        scratch_shapes=[
            pltpu.VMEM(tangent.shape, BF16),
            pltpu.SemaphoreType.DMA((5,)),
            pltpu.SemaphoreType.DMA((5,)),
        ],
    )(tangent_next, port_amp, moved)
    moved = moved.transpose(0, 1, 3, 2)
    return moved, tangent_next, port_amp


def solution(mesh):
    nx, ny = mesh.shape["gx"], mesh.shape["gy"]
    return jax.shard_map(
        functools.partial(per_device, nx, ny),
        mesh=mesh,
        in_specs=(
            P("gx", "gy", None, None),
            P("gx", "gy", None, None),
            P("gx", "gy", None),
            P("gx", "gy", None),
            P("gx", "gy", None),
            P("gx", "gy", None),
            P("gx", "gy", None),
            P("gx", "gy", None, None),
            P("gx", "gy", None),
            P(),
            P("gx", "gy", None),
            P("gx", "gy", None, None),
        ),
        out_specs=(P("gx", "gy", None, None), P("gx", "gy", None), P("gy", "gx")),
        check_vma=False,
    )
```

```python
import functools

import jax
import jax.numpy as jnp
import numpy as np
from jax import lax
from jax.experimental import pallas as pl
from jax.experimental.pallas import tpu as pltpu
from jax.sharding import PartitionSpec as P

PORTS = 64
PORT_DEPTH = 40
EZ = 5
NT = 64
NZN = 26
GLL_POINTS = np.array(
    [-1.0, -0.765055323929465, -0.285231516480645, 0.285231516480645, 0.765055323929465, 1.0]
)
GLL_WEIGHTS = np.array(
    [
        1.0 / 15.0,
        0.378474956297847,
        0.554858377035486,
        0.554858377035486,
        0.378474956297847,
        1.0 / 15.0,
    ]
)
STEP_SQUARED = 0.03
MESH = pl.DeviceIdType.MESH
F32 = jnp.float32
BF16 = jnp.bfloat16
COLS = 3 * NZN * NT
WIDE = COLS + 128
PAIRS = ((0, 1), (2, 3), (5, 6), (7, 8), (4, 9))


def derivative_table():
    identity = np.eye(6)
    differences = GLL_POINTS[:, None] - GLL_POINTS[None, :] + identity
    barycentric = 1.0 / np.prod(differences, axis=1)
    matrix = barycentric[None, :] / barycentric[:, None] / differences
    matrix = matrix * (1.0 - identity)
    matrix = matrix - identity * matrix.sum(axis=1)[:, None]
    return matrix


def split_bf16(table):
    high = table.astype(jnp.bfloat16)
    low = (table - high.astype(np.float64)).astype(jnp.bfloat16)
    return [high, low]


def element_tables():
    d = derivative_table()
    eye = np.eye(6)
    ds = [
        np.kron(np.kron(d, eye), eye),
        np.kron(np.kron(eye, d), eye),
        np.kron(np.kron(eye, eye), d),
    ]
    w = np.kron(np.kron(GLL_WEIGHTS, GLL_WEIGHTS), GLL_WEIGHTS)[:, None]
    lap = sum(m.T @ (w * m) for m in ds)
    both = np.zeros((2, 216, 3, 216, 3))
    for c in range(3):
        for e in range(3):
            both[0, :, c, :, e] = ds[c].T @ (w * ds[e])
            both[1, :, c, :, e] = ds[e].T @ (w * ds[c]) + (lap if c == e else 0.0)
    both = both.reshape(2, 6, 6, 6, 3, 6, 6, 6, 3)
    both = both.transpose(0, 1, 3, 4, 2, 5, 7, 8, 6)
    both = both.reshape(2, 6, 108, 6, 108)
    both = np.pad(both, ((0, 0), (0, 0), (0, 4), (0, 0), (0, 4))).reshape(2, 6, 112, 672)
    both = both.transpose(1, 0, 2, 3).reshape(6, 224, 672)
    return np.concatenate(split_bf16(both), axis=1)


def layout_tables():
    expand = np.zeros((128, NZN, 3, NT))
    for k in range(NZN):
        for c in range(3):
            expand[c * 32 + k, k, c, :] = 1.0
    gather = np.zeros((2, 128, 18, 128))
    for ey in range(2):
        for ez in range(EZ):
            for kz in range(6):
                for c in range(3):
                    gather[ey, c * 32 + 5 * ez + kz, kz * 3 + c, ey * 5 + ez] = 1.0
    gather = gather.reshape(256, 18 * 128)
    return (
        expand.reshape(128, COLS).astype(jnp.bfloat16),
        gather.astype(jnp.bfloat16),
        np.ascontiguousarray(gather.T).astype(jnp.bfloat16),
    )


X_PACK = (
    (np.s_[0:10, 0:3200], np.s_[0:10, 0:3200]),
    (np.s_[10:16, 0:1920], np.s_[0:6, 3200:5120]),
    (np.s_[10:14, 1920:3200], np.s_[6:10, 3200:4480]),
    (np.s_[14:16, 1920:2560], np.s_[6:8, 4480:5120]),
    (np.s_[14:16, 2560:3200], np.s_[8:10, 4480:5120]),
)


def lane_tile(t):
    return slice(t * 128, (t + 1) * 128)


def hi_lo(values):
    high = values.astype(BF16)
    return high, (values - high.astype(F32)).astype(BF16)


def dot(a, b):
    return jnp.dot(a, b, preferred_element_type=F32)


def kernel(
    nx, ny, nsrc_y,
    lam_ref, mu_ref, cell_ref, dir_ref, tan_hbm, tanp_hbm, now, past, load, mode, mass, pid, k_hbm, e_hbm, p_hbm, q_hbm,
    tan_hbm_out, disp_out, port_out,
    tan, tanp, tan_out, out_sem, prep,
    kv, ev, pv, qv, const_sem,
    txf, tpf, exf, wf, oh, oht, uu, ms, ps, dsc, z, o, zf, cf, fs, fpb,
    s1x, s1y, s1d, r1x, r1y, r1d, s2x, s2y, s2d, s2p, r2x, r2y, r2d, r2p,
    pbuf, prec, send_sem, recv_sem, psend, precv,
):
    gx = lax.axis_index("gx")
    gy = lax.axis_index("gy")
    consts = [
        pltpu.make_async_copy(a, b, const_sem.at[i])
        for i, (a, b) in enumerate(
            (
                (e_hbm, ev), (p_hbm, pv), (k_hbm, kv), (q_hbm, qv),
                (tan_hbm, tan), (tanp_hbm, tanp),
            )
        )
    ]
    for i in (4, 5, 0, 1, 2, 3):
        consts[i].start()

    x_lo, x_hi = gx > 0, gx < nx - 1
    y_lo, y_hi = gy > 0, gy < ny - 1
    first_src = ny - nsrc_y
    is_src = gy >= first_src
    n_all = nx * ny
    me = gx * ny + gy

    barrier = pltpu.get_barrier_semaphore()
    around = (
        (x_lo, -1, 0), (x_hi, 1, 0), (y_lo, 0, -1), (y_hi, 0, 1),
        (jnp.logical_and(x_lo, y_lo), -1, -1), (jnp.logical_and(x_hi, y_hi), 1, 1),
    )
    expected = jnp.int32(0)
    for there, dx, dy in around:
        @pl.when(there)
        def _(dx=dx, dy=dy):
            pl.semaphore_signal(barrier, inc=1, device_id=(gx + dx, gy + dy), device_id_type=MESH)
        expected = expected + there.astype(jnp.int32)

    def greet(s, carry):
        sx = s // nsrc_y
        sy = first_src + s % nsrc_y

        @pl.when(sx * ny + sy != me)
        def _():
            pl.semaphore_signal(barrier, inc=1, device_id=(sx, sy), device_id_type=MESH)
        return carry

    lax.fori_loop(0, nx * nsrc_y, greet, 0)
    expected = expected + is_src.astype(jnp.int32) * (n_all - 1)

    def lanes(source, index, x):
        for c in range(3):
            prep[index, x, 0:10, 32 * c:32 * c + NZN] = source[x, :, c, :].astype(F32)

    prep[...] = jnp.zeros_like(prep)
    lanes(now, 0, 0)

    consts[4].wait()
    layer = jnp.concatenate([tan[0], prep[0, 0, 0:10, :].astype(BF16)], axis=1)
    for to, at in X_PACK:
        s1x[to] = layer[at]
    pl.semaphore_wait(barrier, expected)

    def remote(index, src, dst, dx, dy):
        return pltpu.make_async_remote_copy(
            src_ref=src, dst_ref=dst, send_sem=send_sem.at[index], recv_sem=recv_sem.at[index],
            device_id=(gx + dx, gy + dy), device_id_type=MESH,
        )

    first = (
        (remote(0, s1x, r1x, -1, 0), x_lo, x_hi, r1x),
        (remote(1, s1y, r1y, 0, -1), y_lo, y_hi, r1y),
        (remote(2, s1d, r1d, -1, -1), jnp.logical_and(x_lo, y_lo), jnp.logical_and(x_hi, y_hi), r1d),
    )
    second = (
        (remote(3, s2x, r2x, 1, 0), x_hi, x_lo, r2x),
        (remote(4, s2d, r2d, 1, 1), jnp.logical_and(x_hi, y_hi), jnp.logical_and(x_lo, y_lo), r2d),
        (remote(5, s2p, r2p, 0, 1), y_hi, y_lo, r2p),
    ) + tuple(
        (remote(6 + x, s2y.at[x], r2y.at[x], 0, 1), y_hi, y_lo, r2y.at[x]) for x in range(5)
    )

    def start(item):
        copy, sends, _, _ = item

        @pl.when(sends)
        def _():
            copy.start()

    def arrived(item):
        copy, _, receives, buffer = item

        @pl.when(receives)
        def _():
            copy.wait_recv()

        @pl.when(jnp.logical_not(receives))
        def _():
            buffer[...] = jnp.zeros_like(buffer)

    def sent(item):
        copy, sends, _, _ = item

        @pl.when(sends)
        def _():
            copy.wait_send()

    start(first[0])
    s1y[...] = jnp.zeros_like(s1y)
    s1d[...] = jnp.zeros_like(s1d)
    for x in range(5):
        if x > 0:
            lanes(now, 0, x)
        s1y[x:x + 1, 0:COLS] = tan[x, 0:1, :]
        s1y[x:x + 1, COLS:] = prep[0, x, 0:1, :].astype(BF16)
    row = s1y[0:1, :]
    for r in range(14):
        width = min(384, WIDE - r * 384)
        s1d[r:r + 1, 0:width] = row[:, r * 384:r * 384 + width]
    start(first[1])
    start(first[2])

    lane = lax.broadcasted_iota(jnp.int32, (1, 128), 1)
    low_half = lane < 64

    def halves(a, b):
        return jnp.where(low_half, a, b)

    def prepare(x, carry):
        txf[x, 8:16, :] = jnp.zeros((8, WIDE), F32)
        tpf[x, 8:16, :] = jnp.zeros((8, COLS), F32)
        txf[x, 0:10, 0:COLS] = tan[x].astype(F32)
        txf[x, :, COLS:] = prep[0, x]
        for index, source in ((1, past), (2, load), (3, mode)):
            lanes(source, index, x)
        tpf[x, 0:10, :] = tanp[x].astype(F32)
        ms[...] = jnp.ones_like(ms)
        ps[...] = jnp.full(ps.shape, PORTS, jnp.int32)
        ms[0:10, 0:NZN] = mass[x]
        ps[0:10, 0:NZN] = pid[x]
        rep_row = lax.broadcasted_iota(jnp.int32, (128, 128), 0)
        rep_col = lax.broadcasted_iota(jnp.int32, (128, 128), 1)
        rep = jnp.where((rep_col % 32 == rep_row) & (rep_row < NZN), 1.0, 0.0).astype(BF16)
        inv_hi, inv_lo = hi_lo(STEP_SQUARED / ms[...])
        exf[x, 0:16] = dot(inv_hi, rep).astype(BF16)
        exf[x, 16:32] = dot(inv_lo, rep).astype(BF16)
        exf[x, 32:48] = prep[3, x].astype(BF16)
        ids = ps[...]
        rows = pl.ds(pl.multiple_of(x * 16, 16), 16)
        for pair in range(13):
            port = halves(ids[:, 2 * pair:2 * pair + 1], ids[:, 2 * pair + 1:2 * pair + 2])
            oh[pair, rows, :] = jnp.where(port == lane % 64, 1.0, 0.0)
        return carry

    consts[5].wait()
    lax.fori_loop(0, 5, prepare, 0)

    @pl.when(is_src)
    def _():
        oht[...] = oh[...].reshape(1040, 128).T.astype(BF16)

    consts[0].wait()
    lhs = exf[...].reshape(240, 128)

    def widen(n, carry):
        cols = pl.ds(pl.multiple_of(n * 384, 384), 384)
        w = dot(lhs, ev[:, cols]).reshape(5, 48, 384)
        wf[:, 0:16, cols] = w[:, 0:16] + w[:, 16:32]
        wf[:, 16:32, cols] = w[:, 32:48]
        return carry

    lax.fori_loop(0, COLS // 384, widen, 0)

    def gather_points(layers):
        near = jnp.concatenate([txf[x, 0:8, COLS:] for x in layers], axis=0)
        far = jnp.concatenate([txf[x, 5:13, COLS:] for x in layers], axis=0)
        gathered = dot(jnp.concatenate([near, far], axis=1).astype(BF16), pv[...])
        for n, x in enumerate(layers):
            dsc[x] = gathered[8 * n:8 * n + 8]

    arrived(first[1])
    for x in range(5):
        txf[x, 10:11, :] = r1y[x:x + 1, :].astype(F32)
    consts[1].wait()
    gather_points(range(5))

    zf[96:112, :] = jnp.zeros((16, 768), F32)

    def fill(x, carry):
        def tile(m, ey, ez):
            kc = 15 * ez + m
            return txf[x, 5 * ey:5 * ey + 8, lane_tile(kc // 2)]

        for m in range(18):
            rows = slice(6 * m, 6 * m + 8)
            for i, (e1, e2) in enumerate(PAIRS):
                a, b = tile(m, e1 // 5, e1 % 5), tile(m, e2 // 5, e2 % 5)
                a_half, b_half = (15 * (e1 % 5) + m) % 2, (15 * (e2 % 5) + m) % 2
                if a_half == 0 and b_half == 1:
                    both = halves(a, b)
                elif a_half == 1 and b_half == 0:
                    both = pltpu.roll(halves(b, a), 64, 1)
                elif a_half == 0:
                    both = halves(a, pltpu.roll(b, 64, 1))
                else:
                    both = halves(pltpu.roll(a, 64, 1), b)
                zf[rows, lane_tile(i)] = both
            zf[rows, lane_tile(5)] = dsc[x, :, lane_tile(m)]
        z[x] = zf[...].astype(BF16)
        return carry

    lax.fori_loop(0, 5, fill, 0)
    arrived(first[0])
    arrived(first[2])
    txf[5, 8:16, :] = jnp.zeros((8, WIDE), F32)
    for to, at in X_PACK:
        txf[(5,) + at] = r1x[to].astype(F32)
    for r in range(14):
        width = min(384, WIDE - r * 384)
        txf[5, 10:11, r * 384:r * 384 + width] = r1d[r:r + 1, 0:width].astype(F32)
    gather_points([5])
    fill(5, 0)
    consts[2].wait()

    def apply(x):
        rhs = z[...].reshape(672, 768)
        full = dot(kv[x], rhs)
        o[x] = full[0:224] + full[224:448]

    def per_element(values):
        return [values[e // 5:e // 5 + 1, e % 5:e % 5 + 1] for e in range(10)]

    lams = per_element(lam_ref[0].astype(F32))
    mus = per_element(mu_ref[0].astype(F32))
    cells = per_element(cell_ref[0])
    lam_rows = [halves(lams[a], lams[b]) for a, b in PAIRS]
    mu_rows = [halves(mus[a], mus[b]) for a, b in PAIRS]
    lam_point = sum(jnp.where(lane == e, lams[e], 0.0) for e in range(10))
    mu_point = sum(jnp.where(lane == e, mus[e], 0.0) for e in range(10))
    sel_row = lax.broadcasted_iota(jnp.int32, (128, 128), 0)
    direction = jnp.concatenate([dir_ref[...], dir_ref[...]], axis=1)
    choose = jnp.concatenate(
        [
            jnp.where(
                (sel_row == halves(a, b)) & (direction == halves(cells[a], cells[b])), 1.0, 0.0
            ).astype(BF16)
            for a, b in PAIRS
        ],
        axis=1,
    )

    first_row = lax.broadcasted_iota(jnp.int32, (8, 128), 0) == 0

    def merged(pieces):
        low, high = [functools.reduce(jnp.add, p) if p else 0.0 for p in pieces]
        return halves(low, high)

    def assemble(x):
        tile5 = o[x, 112:224, lane_tile(5)]
        cf[0:112, lane_tile(5)] = lam_point * o[x, 0:112, lane_tile(5)] + mu_point * tile5
        point = jnp.concatenate([cf[6 * m:6 * m + 8, lane_tile(5)] for m in range(18)], axis=1)
        point_hi = point.astype(BF16).astype(F32)
        fpb[x] = jnp.concatenate([point_hi, point - point_hi], axis=0).astype(BF16)
        k_hi, k_lo = hi_lo(tile5)
        source = dot(k_hi, choose) + dot(k_lo, choose)
        for i in range(5):
            cf[0:112, lane_tile(i)] = (
                lam_rows[i] * o[x, 0:112, lane_tile(i)]
                + mu_rows[i] * o[x, 112:224, lane_tile(i)]
                + source[:, lane_tile(i)]
            )
        fs[x, 8:16, :] = jnp.zeros((8, WIDE), F32)
        for ey in range(2):
            for t in range(39):
                stay, move = ([], []), ([], [])
                for h in range(2):
                    kc = 2 * t + h
                    ez, m = kc // 15, kc % 15
                    for ez_at, m_at in ((ez, m), (ez - 1, m + 15)):
                        if 0 <= ez_at < EZ and m_at < 18:
                            e = ey * 5 + ez_at
                            i = next(n for n, p in enumerate(PAIRS) if e in p)
                            half = PAIRS[i].index(e)
                            piece = cf[6 * m_at:6 * m_at + 8, lane_tile(i)]
                            (stay if half == h else move)[half].append(piece)
                total = merged(stay)
                if move[0] or move[1]:
                    total = total + pltpu.roll(merged(move), 64, 1)
                if ey == 0:
                    fs[x, 0:8, lane_tile(t)] = total
                else:
                    shared = jnp.where(first_row, fs[x, 5:13, lane_tile(t)], 0.0)
                    fs[x, 5:13, lane_tile(t)] = shared + total

    def place_point(x, values):
        values = values[0:8] + values[8:16]
        fs[x, 0:8, COLS:] = values[:, 0:128]
        shared = jnp.where(first_row, fs[x, 5:13, COLS:], 0.0)
        fs[x, 5:13, COLS:] = shared + values[:, 128:256]

    def pack_row(buffer, values):
        for r in range(-(-values.shape[1] // 384)):
            width = min(384, values.shape[1] - r * 384)
            buffer[r:r + 1, 0:width] = values[:, r * 384:r * 384 + width].astype(BF16)

    s2d[...] = jnp.zeros_like(s2d)
    s2y[...] = jnp.zeros_like(s2y)
    s2p[...] = jnp.zeros_like(s2p)
    apply(5)
    consts[3].wait()
    assemble(5)
    apply(0)
    place_point(5, dot(fpb[5], qv[...]))
    s2x[...] = fs[5].astype(BF16)
    pack_row(s2d, fs[5, 10:11, :])
    start(second[0])
    start(second[1])
    for x in range(5):
        if x < 4:
            apply(x + 1)
        assemble(x)
        pack_row(s2y.at[x], fs[x, 10:11, 0:COLS])
        start(second[3 + x])
    points = dot(fpb[0:5].reshape(80, 18 * 128), qv[...])
    for x in range(5):
        place_point(x, points[16 * x:16 * x + 16])
        s2p[x:x + 1, :] = fs[x, 10:11, COLS:].astype(BF16)
    start(second[2])

    def add_row(x, buffer, width):
        for r in range(-(-width // 384)):
            size = min(384, width - r * 384)
            cols = slice(r * 384, r * 384 + size)
            fs[x, 0:1, cols] = fs[x, 0:1, cols] + buffer[r:r + 1, 0:size].astype(F32)

    def finish(x, carry):
        rows = pl.ds(pl.multiple_of(x * 16, 16), 16)
        for pair in range(13):
            parts = []
            for t in range(3 * pair, 3 * pair + 3):
                cols = lane_tile(t)
                full = 2.0 * txf[x, :, cols] - tpf[x, :, cols] - wf[x, 0:16, cols] * fs[x, :, cols]
                tan_out[x, :, cols] = full[0:10].astype(BF16)
                parts.append(full * wf[x, 16:32, cols])
            a, b, c = parts
            amount = halves(a + pltpu.roll(a, 64, 1), c + pltpu.roll(c, 64, 1)) + b
            high, low = hi_lo(amount)
            uu[pair, rows, 0:128] = high
            uu[pair, rows, 128:256] = low
        return carry

    def finish_points(x, carry):
        fs[x, 0:1, COLS:] = fs[x, 0:1, COLS:] + r2p[x:x + 1, :].astype(F32)
        scale = exf[x, 0:16].astype(F32) + exf[x, 16:32].astype(F32)
        moved = (
            2.0 * txf[x, :, COLS:]
            - prep[1, x]
            + scale * (prep[2, x] - fs[x, :, COLS:])
        )
        for c in range(3):
            disp_out[x, :, c, :] = moved[0:10, 32 * c:32 * c + NZN].astype(BF16)
        return carry

    outs = [
        pltpu.make_async_copy(tan_out.at[x], tan_hbm_out.at[x], out_sem.at[x]) for x in range(5)
    ]
    for x in (1, 2, 3):
        arrived(second[3 + x])
        add_row(x, r2y.at[x], COLS)
    lax.fori_loop(1, 4, finish, 0)
    for x in (1, 2, 3):
        outs[x].start()
    arrived(second[0])
    arrived(second[1])
    arrived(second[3])
    fs[0] = fs[0] + r2x[...].astype(F32)
    add_row(0, r2y.at[0], COLS)
    add_row(0, r2d, WIDE)
    finish(0, 0)
    outs[0].start()
    arrived(second[7])
    add_row(4, r2y.at[4], COLS)
    finish(4, 0)
    outs[4].start()

    per_row = PORTS // ny
    slot = gx * nsrc_y + (gy - first_src)

    def port_copy(target_x, target_y, slot_at):
        return pltpu.make_async_remote_copy(
            src_ref=pbuf.at[target_y], dst_ref=prec.at[slot_at],
            send_sem=psend.at[target_x * ny + target_y], recv_sem=precv.at[slot_at],
            device_id=(target_x, target_y), device_id_type=MESH,
        )

    @pl.when(is_src)
    def _():
        square = dot(oht[...], uu[...].reshape(1040, 256))
        square = square[:, 0:128] + square[:, 128:256]
        amp = square[0:64] + pltpu.roll(square[64:128], 64, 1)
        for g in range(ny):
            pbuf[g] = jnp.zeros((8, 128), F32)
            pbuf[g, 0:per_row, :] = amp[g * per_row:(g + 1) * per_row]

        def send(t, carry):
            @pl.when(t != me)
            def _():
                port_copy(t // ny, t % ny, slot).start()
            return carry

        lax.fori_loop(0, n_all, send, 0)
        prec[slot] = pbuf[gy]

    arrived(second[2])
    for x in range(5):
        finish_points(x, 0)

    def collect(s, acc):
        @pl.when(jnp.logical_or(jnp.logical_not(is_src), s != slot))
        def _():
            port_copy(gx, gy, s).wait_recv()
        return acc + prec[s]

    acc = lax.fori_loop(0, nx * nsrc_y, collect, jnp.zeros((8, 128), F32))
    per_col = NT // nx
    mine = acc[0:per_row, 0:per_col]
    for h in range(1, nx):
        mine = jnp.where(gx == h, acc[0:per_row, h * per_col:(h + 1) * per_col], mine)
    port_out[...] = mine

    for copy in outs:
        copy.wait()
    for item in first + second:
        sent(item)

    @pl.when(is_src)
    def _():
        def drain(t, carry):
            @pl.when(t != me)
            def _():
                port_copy(t // ny, t % ny, slot).wait_send()
            return carry

        lax.fori_loop(0, n_all, drain, 0)


def settle(tan, port, point, tan_out, port_out, point_out):
    tan_out[...] = tan[...]
    port_out[...] = port[...]
    point_out[...] = point[...]


def per_device(
    nx, ny,
    disp, disp_prev, tangent, tangent_prev, lame_lambda, lame_mu, node_mass, force,
    cell_block, direction_block, port_id, port_mode,
):
    rows = disp.shape[1]
    nsrc_y = -(-PORT_DEPTH // rows)
    primal = [a.transpose(0, 1, 3, 2) for a in (disp, disp_prev, force, port_mode)]
    expand, gather, scatter = layout_tables()
    tables = element_tables()
    nsrc = nx * nsrc_y
    vmem = pl.BlockSpec(memory_space=pltpu.VMEM)
    hbm = pl.BlockSpec(memory_space=pl.ANY)
    big = pltpu.VMEM((16, WIDE), BF16)
    small = pltpu.VMEM((16, 384), BF16)
    packed = pltpu.VMEM((16, 3200), BF16)
    rows5 = pltpu.VMEM((5, 16, 384), BF16)
    point = pltpu.VMEM((16, 128), BF16)
    tangent_next, moved, port_amp = pl.pallas_call(
        functools.partial(kernel, nx, ny, nsrc_y),
        out_shape=(
            jax.ShapeDtypeStruct(tangent.shape, BF16),
            jax.ShapeDtypeStruct(primal[0].shape, BF16),
            jax.ShapeDtypeStruct((PORTS // ny, NT // nx), F32),
        ),
        in_specs=[vmem] * 4 + [hbm] * 2 + [vmem] * 6 + [hbm] * 4,
        out_specs=(hbm, vmem, vmem),
        scratch_shapes=[
            pltpu.VMEM(tangent.shape, BF16),
            pltpu.VMEM(tangent.shape, BF16),
            pltpu.VMEM(tangent.shape, BF16),
            pltpu.SemaphoreType.DMA((5,)),
            pltpu.VMEM((4, 5, 16, 128), F32),
            pltpu.VMEM(tables.shape, BF16),
            pltpu.VMEM(expand.shape, BF16),
            pltpu.VMEM(gather.shape, BF16),
            pltpu.VMEM(scatter.shape, BF16),
            pltpu.SemaphoreType.DMA((6,)),
            pltpu.VMEM((6, 16, WIDE), F32),
            pltpu.VMEM((5, 16, COLS), F32),
            pltpu.VMEM((5, 48, 128), BF16),
            pltpu.VMEM((5, 32, COLS), F32),
            pltpu.VMEM((13, 80, 128), F32),
            pltpu.VMEM((128, 1040), BF16),
            pltpu.VMEM((13, 80, 256), BF16),
            pltpu.VMEM((16, 128), F32),
            pltpu.VMEM((16, 128), jnp.int32),
            pltpu.VMEM((6, 8, 18 * 128), F32),
            pltpu.VMEM((6, 112, 768), BF16),
            pltpu.VMEM((6, 224, 768), F32),
            pltpu.VMEM((112, 768), F32),
            pltpu.VMEM((112, 768), F32),
            pltpu.VMEM((6, 16, WIDE), F32),
            pltpu.VMEM((6, 16, 18 * 128), BF16),
            packed, big, small, packed, big, small,
            big, rows5, small, point, big, rows5, small, point,
            pltpu.VMEM((ny, 8, 128), F32),
            pltpu.VMEM((nsrc, 8, 128), F32),
            pltpu.SemaphoreType.DMA((11,)),
            pltpu.SemaphoreType.DMA((11,)),
            pltpu.SemaphoreType.DMA((nx * ny,)),
            pltpu.SemaphoreType.DMA((nsrc,)),
        ],
        compiler_params=pltpu.CompilerParams(
            collective_id=0, has_side_effects=True, vmem_limit_bytes=56 * 1024 * 1024
        ),
    )(
        lame_lambda, lame_mu, cell_block, direction_block[None], tangent, tangent_prev, *primal, node_mass, port_id,
        jnp.asarray(tables), jnp.asarray(expand), jnp.asarray(gather), jnp.asarray(scatter),
    )
    tangent_next, port_amp, moved = pl.pallas_call(
        settle,
        out_shape=(
            jax.ShapeDtypeStruct(tangent_next.shape, BF16),
            jax.ShapeDtypeStruct(port_amp.shape, F32),
            jax.ShapeDtypeStruct(moved.shape, BF16),
        ),
        in_specs=[vmem] * 3,
        out_specs=(vmem, vmem, vmem),
    )(tangent_next, port_amp, moved)
    moved = moved.transpose(0, 1, 3, 2)
    return moved, tangent_next, port_amp


def solution(mesh):
    nx, ny = mesh.shape["gx"], mesh.shape["gy"]
    return jax.shard_map(
        functools.partial(per_device, nx, ny),
        mesh=mesh,
        in_specs=(
            P("gx", "gy", None, None),
            P("gx", "gy", None, None),
            P("gx", "gy", None),
            P("gx", "gy", None),
            P("gx", "gy", None),
            P("gx", "gy", None),
            P("gx", "gy", None),
            P("gx", "gy", None, None),
            P("gx", "gy", None),
            P(),
            P("gx", "gy", None),
            P("gx", "gy", None, None),
        ),
        out_specs=(P("gx", "gy", None, None), P("gx", "gy", None), P("gy", "gx")),
        check_vma=False,
    )
```
